256 devices in a mesh: sector: 32 (over x, y, core), op: 8 (over z).
Axes of the slice: x: 4, y: 4, z: 8, core: 2. Of those that a mesh axis runs over, the one named last changes fastest.
Arguments:
- theta: float32 [128, 128, 128], P('sector'), may hold values from -6 to 6
- left_env: bfloat16 [128, 128, 128, 128], P('sector', 'op'), may hold values from -3 to 3
- right_env: bfloat16 [128, 128, 128, 128], P('sector', 'op'), may hold values from -3 to 3
- perm: int32 [128], replicated, may hold values from 0 to 127, each once
- dims: int32 [128, 2], P('sector'), may hold values from 32 to 128, as said below
Outputs:
- lanczos_vec: float32 [128, 128, 128], P('sector')
- coeffs: float32 [6], replicated
- density: float32 [128, 128, 128], P('sector')
The draws below stay inside these ranges and needn't reach their ends.
Inputs may be any that keep to these rules, and one draw needn't show every extreme that they name: `dims`: each entry is a kept dimension of 32 to 128; the first position has 128 on both sides.
All inputs are finite; a program needn't handle non-finite values.
Results may differ from the reference program's by a relative error of at most 0.012.
Values may be sent and summed in bfloat16 or wider, within the bound.
No kernel may reach another device: no remote copies, remote signals or barrier semaphores. Data moves between devices by JAX's collectives and lax.ppermute only.
A program may use at most 64 MiB of HBM per device.

```python
import math
import jax
import jax.numpy as jnp
from jax import lax

BLK = 128
SEC_DEV = 4
SECTORS = 128
TERMS = 128


def draw_dims(key, part):
    key = jax.random.fold_in(key, 7)
    values = jax.random.randint(key, (SECTORS, 2), BLK // 4, BLK + 1).astype(jnp.int32)
    return values.at[0].set(BLK)


def build_env(spread_part, group_log, block_factor):
    own_count = (TERMS + 1) // 3
    base_amp = jnp.sqrt(jnp.sqrt(jnp.float32(TERMS)) / jnp.float32(own_count))
    group_idx = jnp.arange(SECTORS, dtype=jnp.int32) // SEC_DEV
    amplitude = base_amp * jnp.exp(group_log)[group_idx] * block_factor
    own_terms = (jnp.arange(TERMS, dtype=jnp.int32) % 3 == 1).astype(jnp.float32)
    identity = jnp.eye(BLK, dtype=jnp.float32)
    diagonal = amplitude[:, None, None, None] * own_terms[None, :, None, None] * identity[None, None, :, :]
    return (spread_part / jnp.sqrt(jnp.float32(BLK)) + diagonal).astype(jnp.bfloat16)


def group_ramp(group_key, low_log, high_log):
    groups = SECTORS // SEC_DEV
    frac = jnp.arange(groups, dtype=jnp.float32) / jnp.float32(max(groups - 1, 1))
    jitter = jax.random.uniform(group_key, (groups,), jnp.float32, -0.15, 0.15)
    return low_log + (high_log - low_log) * frac + jitter


def draw_left_env(key, part):
    key = jax.random.fold_in(key, 11)
    noise_key, group_key, block_key = jax.random.split(key, 3)
    shape = (SECTORS, TERMS, BLK, BLK)
    block_factor = jax.random.uniform(block_key, (SECTORS,), jnp.float32, 0.8, 1.2)
    spread_part = jnp.clip(jax.random.normal(noise_key, shape, jnp.float32), -4.0, 4.0)
    group_log = group_ramp(group_key, math.log(0.33), 0.0)
    return build_env(spread_part, group_log, block_factor)


def draw_right_env(key, part):
    key = jax.random.fold_in(key, 13)
    noise_key, group_key, block_key = jax.random.split(key, 3)
    shape = (SECTORS, TERMS, BLK, BLK)
    block_factor = jax.random.uniform(block_key, (SECTORS,), jnp.float32, 0.8, 1.2)
    spread_part = jnp.clip(jax.random.normal(noise_key, shape, jnp.float32), -4.0, 4.0)
    group_log = group_ramp(group_key, math.log(0.33), 0.0)
    return build_env(spread_part, group_log, block_factor)


def levels(rng, shape, cuts, least, largest):
    def one(position, parts):
        steps = jax.random.uniform(jax.random.fold_in(jax.random.fold_in(rng, 6), position), (parts,), jnp.float32, least / len(cuts), largest / len(cuts))
        return jnp.repeat(jnp.exp(steps), shape[position] // parts).reshape((-1,) + (1,) * (len(shape) - position - 1))

    gain = one(*cuts[0])
    for cut in cuts[1:]:
        gain = gain * one(*cut)
    return gain


def noise(key, shape, scale, most, cuts=(), kind=jnp.bfloat16):
    drawn = scale * jax.random.normal(key, shape, jnp.float32)
    if cuts:
        drawn = drawn * levels(key, shape, cuts, -0.22, 0.18)
    return jnp.clip(drawn, -most, most).astype(kind)


def setup_inputs(seed: int = 0) -> dict:
    arg_keys = jax.random.split(jax.random.key(seed), 6)
    return {
        "theta": noise(arg_keys[0], (SECTORS, BLK, BLK), 1.0, 6.0, ((0, 32),), jnp.float32),
        "left_env": draw_left_env(jax.random.fold_in(arg_keys[5], 71), 0),
        "right_env": draw_right_env(jax.random.fold_in(arg_keys[5], 71), 0),
        "perm": jax.random.permutation(arg_keys[3], SECTORS).astype(jnp.int32),
        "dims": draw_dims(jax.random.fold_in(arg_keys[5], 71), 0),
    }


def make_mask(dims):
    rows = jnp.arange(BLK, dtype=jnp.int32)
    inside_rows = (rows[None, :] < dims[:, 0:1]).astype(jnp.float32)
    inside_cols = (rows[None, :] < dims[:, 1:2]).astype(jnp.float32)
    return inside_rows[:, :, None] * inside_cols[:, None, :]

def apply_ham(vec, left_env, right_env, perm, mask):
    pos_of = jnp.argsort(perm).astype(jnp.int32)
    vec_b = vec.astype(jnp.bfloat16)
    shifts = jnp.arange(3, dtype=jnp.int32) - 1
    term_q = jnp.arange(TERMS, dtype=jnp.int32) % 3

    def single(p):
        sector_id = perm[p]
        src = pos_of[(sector_id + shifts) % SECTORS]
        nbrs = vec_b[src].astype(jnp.float32)
        picked = nbrs[term_q]
        inner = jnp.einsum('wij,wjk->wik', left_env[p].astype(jnp.float32), picked, precision=lax.Precision.HIGHEST).astype(jnp.bfloat16)
        return jnp.einsum('wik,wkl->il', inner.astype(jnp.float32), right_env[p].astype(jnp.float32), precision=lax.Precision.HIGHEST)
    total = lax.map(single, jnp.arange(SECTORS, dtype=jnp.int32))
    return total * mask / jnp.sqrt(jnp.float32(TERMS))

def reference(theta, left_env, right_env, perm, dims):
    count = jnp.float32(SECTORS * BLK * BLK)
    mask = make_mask(dims)
    start_vec = theta * mask
    vector = start_vec / jnp.sqrt(jnp.sum(start_vec * start_vec) / count + 1e-06)
    previous = jnp.zeros_like(vector)
    beta = jnp.float32(0.0)
    alphas = []
    betas = []
    for step in range(3):
        image = apply_ham(vector, left_env, right_env, perm, mask)
        alpha = jnp.sum(vector * image) / count
        resid = image - alpha * vector - beta * previous
        beta = jnp.sqrt(jnp.sum(resid * resid) / count + 1e-06)
        previous, vector = (vector, resid / beta)
        alphas.append(alpha)
        betas.append(beta)
    coeffs = jnp.stack(alphas + betas)
    density = jnp.einsum('pij,pkj->pik', vector, vector, precision=lax.Precision.HIGHEST) / BLK
    return (vector, coeffs, density)
```

```python
import jax
import jax.numpy as jnp
from jax import lax
from jax.experimental import pallas as pl
from jax.experimental.pallas import tpu as pltpu
from jax.sharding import PartitionSpec as P

F32 = jnp.float32
BF16 = jnp.bfloat16
BOTH = ("sector", "op")
W = 128
SEC = 4
SLAB = 8
NZ = 8
CHIPS = 16
GRP = 16
NBLK = 3 * SEC
TERMS_DEV = 16
COUNT = float(128 * W * W)
EPS = 1e-06
SCALE = 1.0 / (128.0**0.5)
NCOL = 4

CZ_GROUPS = [[(2 * chip + c) * NZ + z for c in range(2) for z in range(NZ)] for chip in range(CHIPS)]
XY_GROUPS = [[2 * chip + c for chip in range(CHIPS)] for c in range(2)]
SWAP = [(i, i ^ 1) for i in range(2 * CHIPS)]

VMEM = pl.BlockSpec(memory_space=pltpu.VMEM)
SMEM = pl.BlockSpec(memory_space=pltpu.SMEM)


def core_and_z():
    return lax.rem(lax.axis_index("sector"), 2), lax.axis_index("op")


def call(body, outs, specs, scratch=(), flops=0, nbytes=1 << 18):
    return pl.pallas_call(
        body,
        out_shape=[jax.ShapeDtypeStruct(s, d) for s, d in outs],
        in_specs=specs,
        out_specs=[VMEM] * len(outs),
        scratch_shapes=list(scratch),
        compiler_params=pltpu.CompilerParams(vmem_limit_bytes=32 * 1024 * 1024),
        cost_estimate=pl.CostEstimate(flops=flops, bytes_accessed=nbytes, transcendentals=0),
    )


def iota(shape, dim):
    return lax.broadcasted_iota(jnp.int32, shape, dim)


def row_sum(x):
    return jnp.sum(x, axis=0, keepdims=True)


def split_rows(rows):
    at = iota((16, W), 0)
    tile = jnp.zeros((16, W), F32)
    for k, row in enumerate(rows):
        hi = row.astype(BF16).astype(F32)
        mid = (row - hi).astype(BF16).astype(F32)
        low = row - hi - mid
        for n, part in enumerate((hi, mid, low)):
            tile = jnp.where(at == 3 * k + n, jnp.broadcast_to(part, (16, W)), tile)
    return tile.astype(BF16)


def join_rows(tile, count):
    return [row_sum(tile[3 * k : 3 * k + 3]) for k in range(count)]


def total(row):
    return jnp.sum(row, axis=1, keepdims=True)


def start_kernel(dims, theta, keep, send):
    c, z = core_and_z()
    for slot, out in ((c * NZ + z, keep), ((1 - c) * NZ + z, send)):
        first = pl.multiple_of(slot * SLAB, SLAB)
        rows = iota((SLAB, W), 0) + first
        cols = iota((SLAB, W), 1)
        for i in range(SEC):
            inside = (rows < dims[i, 0]) & (cols < dims[i, 1])
            out[SLAB * i : SLAB * (i + 1), :] = jnp.where(inside, theta[i, pl.ds(first, SLAB), :], 0.0)


def spread_start_kernel(keep, came, msg, slab):
    c, _ = core_and_z()
    half = SEC * SLAB

    @pl.when(c == 0)
    def _():
        slab[:half] = keep[...]
        slab[half:] = came[...]

    @pl.when(c == 1)
    def _():
        slab[:half] = came[...]
        slab[half:] = keep[...]

    rounded = slab[...].astype(BF16)
    for n in range(CHIPS):
        msg[n] = rounded


def source_kernel(perm, src, pos):
    chip = lax.axis_index("sector") // 2

    def put(p, carry):
        pos[perm[p]] = p
        return carry

    lax.fori_loop(0, 128, put, 0)
    for n in range(2 * SEC):
        mine = perm[chip * 2 * SEC + n]
        for q in range(3):
            src[3 * n + q] = pos[lax.rem(mine + (q + 127), 128)]


def select_kernel(rows, src, got, msg, blocks):
    for n in range(CHIPS):
        blocks[2 * SEC * SLAB * n : 2 * SEC * SLAB * (n + 1)] = got[n, : 2 * SEC * SLAB].astype(F32)
    for c in range(2):
        for pair in range(NBLK // 2):
            two = [
                blocks[pl.ds(pl.multiple_of(src[NBLK * c + 2 * pair + k] * SLAB, SLAB), SLAB), :]
                for k in range(2)
            ]
            tile = jnp.concatenate(two, axis=0).astype(BF16)
            for z in range(NZ):
                msg[c * NZ + z, 16 * pair : 16 * (pair + 1)] = tile
    if rows:
        acc = got[0, 2 * SEC * SLAB :].astype(F32)
        for n in range(1, CHIPS):
            acc = acc + got[n, 2 * SEC * SLAB :].astype(F32)
        tile = split_rows(join_rows(acc, rows))
        for s in range(GRP):
            msg[s, NBLK * SLAB :] = tile


def gathered_totals(got, rows):
    acc = got[0, NBLK * SLAB :].astype(F32)
    for s in range(1, GRP):
        acc = acc + got[s, NBLK * SLAB :].astype(F32)
    return [total(r) for r in join_rows(acc, rows)]


def assemble(got, out):
    for s in range(GRP):
        for pair in range(NBLK // 2):
            tile = got[s, 16 * pair : 16 * (pair + 1)].astype(F32)
            for k in range(2):
                out[2 * pair + k, SLAB * s : SLAB * (s + 1), :] = tile[SLAB * k : SLAB * (k + 1)]


def products(dims, blocks, left, right, msg, acc):
    _, z = core_and_z()
    rows = iota((W, W), 0)
    cols = iota((W, W), 1)
    for i in range(SEC):
        inner = []
        order = []
        for r in range(3):
            terms = list(range(r, TERMS_DEV, 3))
            vec = blocks[3 * i + lax.rem(z + r, 3)].astype(BF16)
            lhs = jnp.concatenate([left[i, w] for w in terms], axis=0)
            got = jnp.dot(lhs, vec, preferred_element_type=F32).astype(BF16)
            inner += [got[W * n : W * (n + 1)] for n in range(len(terms))]
            order += terms
        lhs = jnp.concatenate(inner, axis=1)
        rhs = jnp.concatenate([right[i, w] for w in order], axis=0)
        out = jnp.dot(lhs, rhs, preferred_element_type=F32)
        inside = (rows < dims[i, 0]) & (cols < dims[i, 1])
        acc[i] = jnp.where(inside, out * SCALE, 0.0)
    for s in range(GRP):
        at = slice(SLAB * s, SLAB * (s + 1))
        for pair in range(SEC // 2):
            tile = jnp.concatenate([acc[2 * pair, at, :], acc[2 * pair + 1, at, :]], axis=0)
            msg[s, 16 * pair : 16 * (pair + 1)] = tile.astype(BF16)


def put_coefs(out, values):
    at = iota((8, W), 0)
    tile = jnp.zeros((8, W), F32)
    for k, v in enumerate(values):
        tile = jnp.where(at == k, jnp.broadcast_to(v, (8, W)), tile)
    out[...] = tile


def coef(ref, k):
    return ref[k : k + 1, 0:1]


def ham0_kernel(dims, got, left, right, msg, blk, acc):
    assemble(got, blk)
    products(dims, blk, left, right, msg, acc)


def ham1_kernel(dims, got, left, right, blk0, slab0, image0, msg, blk, v0, v1, coefs, acc):
    uu, uw, ww = gathered_totals(got, 3)
    assemble(got, blk)
    n2 = uu / COUNT + EPS
    inv = 1.0 / jnp.sqrt(n2)
    a0 = uw / n2 / COUNT
    rr = (ww - 2.0 * a0 * uw + a0 * a0 * uu) / n2
    b1 = jnp.sqrt(jnp.maximum(rr, 0.0) / COUNT + EPS)
    wc = inv / b1
    vc = a0 * wc
    for n in range(NBLK):
        blk[n] = blk[n] * wc - blk0[n] * vc
    v0[...] = slab0[...] * inv
    v1[...] = image0[...] * wc - slab0[...] * vc
    put_coefs(coefs, (a0, b1, inv))
    products(dims, blk, left, right, msg, acc)


def ham2_kernel(
    dims, got, left, right, blk1, blk0, slab1, rest1, old, msg, own, v2, coefs, blk, acc
):
    vw, vr, rr, vv = gathered_totals(got, 4)
    assemble(got, blk)
    a0, b1, inv = coef(old, 0), coef(old, 1), coef(old, 2)
    a1 = vw / COUNT
    d = a1 - a0
    rest = rr - 2.0 * d * vr + d * d * vv
    b2 = jnp.sqrt(jnp.maximum(rest, 0.0) / COUNT + EPS)
    wc = 1.0 / b2
    vc = a1 * wc
    pc = b1 * inv * wc
    for n in range(NBLK):
        blk[n] = blk[n] * wc - blk1[n] * vc - blk0[n] * pc
    for i in range(SEC):
        own[i] = blk[3 * i + 1]
    v2[...] = (rest1[...] - d * slab1[...]) * wc
    put_coefs(coefs, (a0, a1, b1, b2))
    products(dims, blk, left, right, msg, acc)


def reduced(got):
    parts = []
    for c in range(2):
        acc = got[c * NZ].astype(F32)
        for z in range(1, NZ):
            acc = acc + got[c * NZ + z].astype(F32)
        parts.append(acc)
    return jnp.concatenate(parts, axis=0)


def spread(msg, image, rows):
    msg_rows = 2 * SEC * SLAB
    rounded = image.astype(BF16)
    tile = split_rows(rows)
    for n in range(CHIPS):
        msg[n, :msg_rows] = rounded
        msg[n, msg_rows:] = tile


def reduce0_kernel(got, slab0, msg, image0):
    image = reduced(got)
    image0[...] = image
    vec = slab0[...]
    spread(msg, image, [row_sum(vec * vec), row_sum(vec * image), row_sum(image * image)])


def inner_rows(vec, image, rest):
    return [row_sum(vec * image), row_sum(vec * rest), row_sum(rest * rest), row_sum(vec * vec)]


def reduce1_kernel(got, v1, v0, coefs, msg, rest1):
    image = reduced(got)
    vec = v1[...]
    rest = image - coef(coefs, 1) * v0[...] - coef(coefs, 0) * vec
    rest1[...] = rest
    spread(msg, image, inner_rows(vec, image, rest))


def reduce2_kernel(got, v2, v1, coefs, msg):
    image = reduced(got)
    vec = v2[...]
    rest = image - coef(coefs, 3) * v1[...] - coef(coefs, 1) * vec
    half = SEC * SLAB
    rows = inner_rows(vec, image, rest)
    at = iota((8, W), 0)
    tile = jnp.zeros((8, W), F32)
    for k, row in enumerate(rows):
        tile = jnp.where(at == k, jnp.broadcast_to(row, (8, W)), tile)
    for c in range(2):
        for z in range(NZ):
            msg[c * NZ + z, :half] = rest[half * c : half * (c + 1)]
            msg[c * NZ + z, half:] = tile


def sums_kernel(got, msg):
    half = SEC * SLAB
    acc = got[0, half:]
    for s in range(1, GRP):
        acc = acc + got[s, half:]
    for n in range(CHIPS):
        msg[n] = acc


def finish_kernel(got, sums, own, coefs, vec_out, coef_out, dens_out):
    acc = sums[0]
    for n in range(1, CHIPS):
        acc = acc + sums[n]
    vw, vr, rr, vv = [total(acc[k : k + 1]) for k in range(4)]
    a0, a1, b1, b2 = [coef(coefs, k) for k in range(4)]
    a2 = vw / COUNT
    d = a2 - a1
    rest = rr - 2.0 * d * vr + d * d * vv
    b3 = jnp.sqrt(jnp.maximum(rest, 0.0) / COUNT + EPS)
    put_coefs(coef_out, (a0, a1, a2, b1, b2, b3))
    wc = 1.0 / b3
    vc = d * wc
    for i in range(SEC):
        for s in range(GRP):
            at = slice(SLAB * s, SLAB * (s + 1))
            vec_out[i, at, :] = got[s, SLAB * i : SLAB * (i + 1)] * wc - own[i, at, :] * vc
        v = vec_out[i]
        dens_out[i] = (
            lax.dot_general(
                v, v, (((1,), (1,)), ((), ())), precision=lax.Precision.HIGHEST, preferred_element_type=F32
            )
            / W
        )


def over_cz(x):
    return lax.all_to_all(x, BOTH, 0, 0, axis_index_groups=CZ_GROUPS)


def over_xy(x):
    return lax.all_to_all(x, "sector", 0, 0, axis_index_groups=XY_GROUPS)


def select(rows, got, src):
    extra = 16 if rows else 0
    return call(
        lambda *refs: select_kernel(rows, *refs),
        [((GRP, NBLK * SLAB + extra, W), BF16)],
        [SMEM, VMEM],
        [pltpu.VMEM((8 * SEC * GRP * 2, W), F32)],
    )(src, got)[0]


def per_device(theta, left, right, perm, dims):
    half = (SEC * SLAB, W)
    slab = (2 * SEC * SLAB, W)
    scatter = ((GRP, SEC * SLAB, W), BF16)
    plane = ((CHIPS, 2 * SEC * SLAB + 16, W), BF16)
    blocks = ((NBLK, W, W), F32)
    acc = [pltpu.VMEM((SEC, W, W), F32)]
    coefs = ((8, W), F32)
    flops = 2 * 2 * SEC * TERMS_DEV * W**3
    nbytes = 6 << 20

    src = pl.pallas_call(
        source_kernel,
        out_shape=jax.ShapeDtypeStruct((6 * SEC,), jnp.int32),
        in_specs=[SMEM],
        out_specs=SMEM,
        scratch_shapes=[pltpu.SMEM((128,), jnp.int32)],
    )(perm)

    keep, send = call(start_kernel, [(half, F32)] * 2, [SMEM, VMEM])(dims, theta)
    came = lax.ppermute(send, "sector", SWAP)
    msg, slab0 = call(
        spread_start_kernel, [((CHIPS, 2 * SEC * SLAB, W), BF16), (slab, F32)], [VMEM, VMEM]
    )(keep, came)
    got = over_cz(select(0, over_xy(msg), src))
    msg, blk0 = call(
        ham0_kernel, [scatter, blocks], [SMEM, VMEM, VMEM, VMEM], acc, flops, nbytes
    )(dims, got, left, right)
    msg, image0 = call(reduce0_kernel, [plane, (slab, F32)], [VMEM] * 2)(over_cz(msg), slab0)

    got = over_cz(select(3, over_xy(msg), src))
    msg, blk1, v0, v1, co = call(
        ham1_kernel,
        [scatter, blocks, (slab, F32), (slab, F32), coefs],
        [SMEM] + [VMEM] * 6,
        acc,
        flops,
        nbytes,
    )(dims, got, left, right, blk0, slab0, image0)
    msg, rest1 = call(reduce1_kernel, [plane, (slab, F32)], [VMEM] * 4)(over_cz(msg), v1, v0, co)

    got = over_cz(select(4, over_xy(msg), src))
    msg, own, v2, co = call(
        ham2_kernel,
        [scatter, ((SEC, W, W), F32), (slab, F32), coefs],
        [SMEM] + [VMEM] * 8,
        [pltpu.VMEM((NBLK, W, W), F32)] + acc,
        flops,
        nbytes,
    )(dims, got, left, right, blk1, blk0, v1, rest1, co)
    (msg,) = call(reduce2_kernel, [((GRP, SEC * SLAB + 8, W), F32)], [VMEM] * 4)(
        over_cz(msg), v2, v1, co
    )

    got = over_cz(msg)
    (msg,) = call(sums_kernel, [((CHIPS, 8, W), F32)], [VMEM])(got)
    vec, coef_tile, dens = call(
        finish_kernel, [((SEC, W, W), F32), coefs, ((SEC, W, W), F32)], [VMEM] * 4
    )(got, over_xy(msg), own, co)
    return vec, coef_tile[:6, 0], dens


def solution(mesh):
    placed = (
        P("sector", None, None),
        P("sector", "op", None, None),
        P("sector", "op", None, None),
        P(),
        P("sector", None),
    )
    return jax.shard_map(
        per_device,
        mesh=mesh,
        in_specs=placed,
        out_specs=(P("sector", None, None), P(), P("sector", None, None)),
        check_vma=False,
    )
```

```python
import jax
import jax.numpy as jnp
from jax import lax
from jax.experimental import pallas as pl
from jax.experimental.pallas import tpu as pltpu
from jax.sharding import PartitionSpec as P

F32 = jnp.float32
BF16 = jnp.bfloat16
BOTH = ("sector", "op")
W = 128
SEC = 4
SLAB = 8
NZ = 8
CHIPS = 16
GRP = 16
NBLK = 3 * SEC
TERMS_DEV = 16
COUNT = float(128 * W * W)
EPS = 1e-06
SCALE = 1.0 / (128.0**0.5)
NCOL = 4

CZ_GROUPS = [[(2 * chip + c) * NZ + z for c in range(2) for z in range(NZ)] for chip in range(CHIPS)]
XY_GROUPS = [[2 * chip + c for chip in range(CHIPS)] for c in range(2)]
SWAP = [(i, i ^ 1) for i in range(2 * CHIPS)]

VMEM = pl.BlockSpec(memory_space=pltpu.VMEM)
SMEM = pl.BlockSpec(memory_space=pltpu.SMEM)


def core_and_z():
    return lax.rem(lax.axis_index("sector"), 2), lax.axis_index("op")


def call(body, outs, specs, scratch=(), flops=0, nbytes=1 << 18, out_specs=None, limit=8):
    return pl.pallas_call(
        body,
        out_shape=[jax.ShapeDtypeStruct(s, d) for s, d in outs],
        in_specs=specs,
        out_specs=out_specs or [VMEM] * len(outs),
        scratch_shapes=list(scratch),
        compiler_params=pltpu.CompilerParams(vmem_limit_bytes=limit << 20),
        cost_estimate=pl.CostEstimate(flops=flops, bytes_accessed=nbytes, transcendentals=0),
    )


def iota(shape, dim):
    return lax.broadcasted_iota(jnp.int32, shape, dim)


def row_sum(x):
    return jnp.sum(x, axis=0, keepdims=True)


def split_rows(rows):
    at = iota((16, W), 0)
    tile = jnp.zeros((16, W), F32)
    for k, row in enumerate(rows):
        hi = row.astype(BF16).astype(F32)
        mid = (row - hi).astype(BF16).astype(F32)
        low = row - hi - mid
        for n, part in enumerate((hi, mid, low)):
            tile = jnp.where(at == 3 * k + n, jnp.broadcast_to(part, (16, W)), tile)
    return tile.astype(BF16)


def join_rows(tile, count):
    return [row_sum(tile[3 * k : 3 * k + 3]) for k in range(count)]


def total(row):
    return jnp.sum(row, axis=1, keepdims=True)


def low_high(low, high):
    first = iota((SLAB, W), 0) < 4
    return (
        jnp.where(first, low, pltpu.roll(high, 4, 0)),
        jnp.where(first, pltpu.roll(low, 4, 0), high),
    )


def start_kernel(theta, dims, msg, keep, send, held, sizes, sems):
    size_copy = pltpu.make_async_copy(dims, sizes, sems.at[SEC])
    copies = [pltpu.make_async_copy(theta.at[i], held.at[i], sems.at[i]) for i in range(SEC)]
    size_copy.start()
    for copy in copies:
        copy.start()
    size_copy.wait()
    rows = iota((W, W), 0)
    cols = iota((W, W), 1)
    for i in range(SEC):
        copies[i].wait()
        inside = (rows < sizes[0, i]) & (cols < sizes[1, i])
        held[i] = jnp.where(inside, held[i], 0.0)
    for t in range(GRP):
        tiles = [held[i, SLAB * t : SLAB * (t + 1), :] for i in range(SEC)]
        even0, odd0 = low_high(tiles[0], tiles[1])
        even1, odd1 = low_high(tiles[2], tiles[3])
        msg[2 * t] = jnp.concatenate([even0, even1], axis=0).astype(BF16)
        msg[2 * t + 1] = jnp.concatenate([odd0, odd1], axis=0).astype(BF16)
    c, z = core_and_z()
    for slot, out in ((c * NZ + z, keep), ((1 - c) * NZ + z, send)):
        first = pl.multiple_of(slot * SLAB, SLAB)
        for i in range(SEC):
            out[SLAB * i : SLAB * (i + 1), :] = held[i, pl.ds(first, SLAB), :]


def load_kernel(array, held, sems):
    copies = [pltpu.make_async_copy(array.at[i], held.at[i], sems.at[i]) for i in range(SEC)]
    for copy in copies:
        copy.start()
    for copy in copies:
        copy.wait()


def hits_kernel(perm, hits):
    shape = (3 * W, W)
    row = iota(shape, 0)
    at = lax.shift_right_logical(row * 21846, 16)
    q = row - 3 * at
    held = jnp.broadcast_to(perm[...], shape)
    mine = jnp.sum(jnp.where(iota(shape, 1) == at, held, 0.0), axis=1, keepdims=True)
    want = mine + q.astype(F32) - 1.0
    want = jnp.where(want < 0.0, want + 128.0, want)
    want = jnp.where(want > 127.0, want - 128.0, want)
    hits[...] = (held == want).astype(F32).astype(BF16)


def pick_kernel(got, hits, src, came, held, msg, pieces, picked):
    for g in range(2 * CHIPS):
        pieces[16 * g : 16 * (g + 1)] = got[g].astype(F32)
    for r in range(4):
        part = pieces[pl.ds(r, W, stride=4), :].astype(BF16)
        picked[pl.ds(r, 3 * W, stride=4), :] = jnp.dot(hits[...], part, preferred_element_type=F32)
    for g in range(2 * CHIPS):
        msg[g] = picked[48 * g : 48 * (g + 1)].astype(BF16)


def assemble_pieces(got, out):
    for t in range(GRP):
        low = got[2 * t].astype(F32)
        high = got[2 * t + 1].astype(F32)
        for m in range(NBLK // 2):
            at = slice(SLAB * m, SLAB * (m + 1))
            two = low_high(low[at], high[at])
            for k in range(2):
                out[2 * m + k, SLAB * t : SLAB * (t + 1), :] = two[k]


def source_kernel(perm, src, pos):
    chip = lax.axis_index("sector") // 2

    def put(p, carry):
        pos[perm[p]] = p
        return carry

    lax.fori_loop(0, 128, put, 0)
    for n in range(2 * SEC):
        mine = perm[chip * 2 * SEC + n]
        for q in range(3):
            src[3 * n + q] = pos[lax.rem(mine + (q + 127), 128)]


def select_kernel(rows, src, got, msg):
    for c in range(2):
        for pair in range(NBLK // 2):
            two = []
            for k in range(2):
                at = src[NBLK * c + 2 * pair + k]
                inner = lax.bitwise_and(at, 7)
                first = pl.multiple_of(lax.shift_right_logical(inner, 1) * 16, 16)
                tile = got[lax.shift_right_logical(at, 3), pl.ds(first, 16), :].astype(F32)
                two.append(jnp.where(lax.bitwise_and(inner, 1) == 1, tile[SLAB:], tile[:SLAB]))
            tile = jnp.concatenate(two, axis=0).astype(BF16)
            for z in range(NZ):
                msg[c * NZ + z, 16 * pair : 16 * (pair + 1)] = tile
    if rows:
        acc = got[0, 2 * SEC * SLAB :].astype(F32)
        for n in range(1, CHIPS):
            acc = acc + got[n, 2 * SEC * SLAB :].astype(F32)
        tile = split_rows(join_rows(acc, rows))
        for s in range(GRP):
            msg[s, NBLK * SLAB :] = tile


def gathered_totals(got, rows):
    acc = got[0, NBLK * SLAB :].astype(F32)
    for s in range(1, GRP):
        acc = acc + got[s, NBLK * SLAB :].astype(F32)
    return [total(r) for r in join_rows(acc, rows)]


def assemble(got, out):
    for s in range(GRP):
        for pair in range(NBLK // 2):
            tile = got[s, 16 * pair : 16 * (pair + 1)].astype(F32)
            for k in range(2):
                out[2 * pair + k, SLAB * s : SLAB * (s + 1), :] = tile[SLAB * k : SLAB * (k + 1)]


def products(dims, blocks, left, right, msg, acc):
    _, z = core_and_z()
    rows = iota((W, W), 0)
    cols = iota((W, W), 1)
    for i in range(SEC):
        inner = []
        order = []
        for r in range(3):
            terms = list(range(r, TERMS_DEV, 3))
            vec = blocks[3 * i + lax.rem(z + r, 3)].astype(BF16)
            lhs = jnp.concatenate([left[i, w] for w in terms], axis=0)
            got = jnp.dot(lhs, vec, preferred_element_type=F32).astype(BF16)
            inner += [got[W * n : W * (n + 1)] for n in range(len(terms))]
            order += terms
        lhs = jnp.concatenate(inner, axis=1)
        rhs = jnp.concatenate([right[i, w] for w in order], axis=0)
        out = jnp.dot(lhs, rhs, preferred_element_type=F32)
        inside = (rows < dims[0, i]) & (cols < dims[1, i])
        acc[i] = jnp.where(inside, out * SCALE, 0.0)
    for s in range(GRP):
        at = slice(SLAB * s, SLAB * (s + 1))
        for pair in range(SEC // 2):
            tile = jnp.concatenate([acc[2 * pair, at, :], acc[2 * pair + 1, at, :]], axis=0)
            msg[s, 16 * pair : 16 * (pair + 1)] = tile.astype(BF16)


def put_coefs(out, values):
    at = iota((8, W), 0)
    tile = jnp.zeros((8, W), F32)
    for k, v in enumerate(values):
        tile = jnp.where(at == k, jnp.broadcast_to(v, (8, W)), tile)
    out[...] = tile


def coef(ref, k):
    return ref[k : k + 1, 0:1]


def ham0_kernel(dims, got, left, right, msg, blk, acc):
    assemble_pieces(got, blk)
    products(dims, blk, left, right, msg, acc)


def ham1_kernel(dims, got, left, right, blk0, slab0, image0, msg, blk, v0, v1, coefs, acc):
    uu, uw, ww = gathered_totals(got, 3)
    assemble(got, blk)
    n2 = uu / COUNT + EPS
    inv = 1.0 / jnp.sqrt(n2)
    a0 = uw / n2 / COUNT
    rr = (ww - 2.0 * a0 * uw + a0 * a0 * uu) / n2
    b1 = jnp.sqrt(jnp.maximum(rr, 0.0) / COUNT + EPS)
    wc = inv / b1
    vc = a0 * wc
    for n in range(NBLK):
        blk[n] = blk[n] * wc - blk0[n] * vc
    v0[...] = slab0[...] * inv
    v1[...] = image0[...] * wc - slab0[...] * vc
    put_coefs(coefs, (a0, b1, inv))
    products(dims, blk, left, right, msg, acc)


def ham2_kernel(
    dims, got, left, right, blk1, blk0, slab1, rest1, old, msg, own, v2, coefs, blk, acc
):
    vw, vr, rr, vv = gathered_totals(got, 4)
    assemble(got, blk)
    a0, b1, inv = coef(old, 0), coef(old, 1), coef(old, 2)
    a1 = vw / COUNT
    d = a1 - a0
    rest = rr - 2.0 * d * vr + d * d * vv
    b2 = jnp.sqrt(jnp.maximum(rest, 0.0) / COUNT + EPS)
    wc = 1.0 / b2
    vc = a1 * wc
    pc = b1 * inv * wc
    for n in range(NBLK):
        blk[n] = blk[n] * wc - blk1[n] * vc - blk0[n] * pc
    for i in range(SEC):
        own[i] = blk[3 * i + 1]
    v2[...] = (rest1[...] - d * slab1[...]) * wc
    put_coefs(coefs, (a0, a1, b1, b2))
    products(dims, blk, left, right, msg, acc)


def reduced(got):
    parts = []
    for c in range(2):
        acc = got[c * NZ].astype(F32)
        for z in range(1, NZ):
            acc = acc + got[c * NZ + z].astype(F32)
        parts.append(acc)
    return jnp.concatenate(parts, axis=0)


def spread(msg, image, rows):
    msg_rows = 2 * SEC * SLAB
    rounded = image.astype(BF16)
    tile = split_rows(rows)
    for n in range(CHIPS):
        msg[n, :msg_rows] = rounded
        msg[n, msg_rows:] = tile


def reduce0_kernel(got, keep, came, msg, image0, slab0):
    c, _ = core_and_z()
    image = reduced(got)
    image0[...] = image
    half = SEC * SLAB
    slab0[:half] = jnp.where(c == 0, keep[...], came[...])
    slab0[half:] = jnp.where(c == 0, came[...], keep[...])
    vec = slab0[...]
    spread(msg, image, [row_sum(vec * vec), row_sum(vec * image), row_sum(image * image)])


def inner_rows(vec, image, rest):
    return [row_sum(vec * image), row_sum(vec * rest), row_sum(rest * rest), row_sum(vec * vec)]


def reduce1_kernel(got, v1, v0, coefs, msg, rest1):
    image = reduced(got)
    vec = v1[...]
    rest = image - coef(coefs, 1) * v0[...] - coef(coefs, 0) * vec
    rest1[...] = rest
    spread(msg, image, inner_rows(vec, image, rest))


def reduce2_kernel(got, v2, v1, coefs, msg):
    image = reduced(got)
    vec = v2[...]
    rest = image - coef(coefs, 3) * v1[...] - coef(coefs, 1) * vec
    half = SEC * SLAB
    tile = split_rows(inner_rows(vec, image, rest))
    for c in range(2):
        rounded = rest[half * c : half * (c + 1)].astype(BF16)
        for z in range(NZ):
            msg[c * NZ + z, :half] = rounded
            msg[c * NZ + z, half:] = tile


def sums_kernel(got, msg):
    half = SEC * SLAB
    acc = got[0, half:].astype(F32)
    for s in range(1, GRP):
        acc = acc + got[s, half:].astype(F32)
    at = iota((8, W), 0)
    tile = jnp.zeros((8, W), F32)
    for k, row in enumerate(join_rows(acc, 4)):
        tile = jnp.where(at == k, jnp.broadcast_to(row, (8, W)), tile)
    for n in range(CHIPS):
        msg[n] = tile


def finish_kernel(got, sums, own, coefs, vec_out, coef_out, dens_out, rest2):
    acc = sums[0]
    for n in range(1, CHIPS):
        acc = acc + sums[n]
    vw, vr, rr, vv = [total(acc[k : k + 1]) for k in range(4)]
    a0, a1, b1, b2 = [coef(coefs, k) for k in range(4)]
    a2 = vw / COUNT
    d = a2 - a1
    rest = rr - 2.0 * d * vr + d * d * vv
    b3 = jnp.sqrt(jnp.maximum(rest, 0.0) / COUNT + EPS)
    for k, v in enumerate((a0, a1, a2, b1, b2, b3)):
        coef_out[k] = v[0, 0]
    wc = 1.0 / b3
    vc = d * wc
    for s in range(GRP):
        for pair in range(SEC // 2):
            tile = got[s, 16 * pair : 16 * (pair + 1)].astype(F32)
            for k in range(2):
                rest2[2 * pair + k, SLAB * s : SLAB * (s + 1), :] = tile[SLAB * k : SLAB * (k + 1)]
    for i in range(SEC):
        v = rest2[i] * wc - own[i] * vc
        vec_out[i] = v
        dens_out[i] = (
            lax.dot_general(
                v, v, (((1,), (1,)), ((), ())), precision=lax.Precision.HIGHEST, preferred_element_type=F32
            )
            / W
        )


def over_cz(x):
    return lax.all_to_all(x, BOTH, 0, 0, axis_index_groups=CZ_GROUPS)


def over_xy(x):
    return lax.all_to_all(x, "sector", 0, 0, axis_index_groups=XY_GROUPS)


def select(rows, got, src):
    extra = 16 if rows else 0
    return call(
        lambda *refs: select_kernel(rows, *refs),
        [((GRP, NBLK * SLAB + extra, W), BF16)],
        [SMEM, VMEM],
    )(src, got)[0]


def per_device(theta, left, right, perm, dims):
    half = (SEC * SLAB, W)
    slab = (2 * SEC * SLAB, W)
    scatter = ((GRP, SEC * SLAB, W), BF16)
    plane = ((CHIPS, 2 * SEC * SLAB + 16, W), BF16)
    blocks = ((NBLK, W, W), F32)
    acc = [pltpu.VMEM((SEC, W, W), F32)]
    coefs = ((8, W), F32)
    flops = 2 * 2 * SEC * TERMS_DEV * W**3
    nbytes = 6 << 20

    dims = dims.T
    any_space = pl.BlockSpec(memory_space=pl.ANY)
    pieces = 2 * CHIPS
    sems = pltpu.SemaphoreType.DMA((SEC + 1,))

    msg, keep, send = call(
        start_kernel,
        [((pieces, 16, W), BF16), (half, F32), (half, F32)],
        [any_space, any_space],
        [pltpu.VMEM((SEC, W, W), F32), pltpu.SMEM((2, SEC), jnp.int32), sems],
        limit=60,
    )(theta, dims)
    got = lax.all_to_all(msg, "sector", 0, 0)
    (hits,) = call(hits_kernel, [((3 * W, W), BF16)], [VMEM])(perm.astype(F32).reshape(1, W))
    (src,) = call(
        source_kernel,
        [((6 * SEC,), jnp.int32)],
        [SMEM],
        [pltpu.SMEM((128,), jnp.int32)],
        out_specs=[SMEM],
        limit=1,
    )(perm)
    (right,) = call(load_kernel, [((SEC, TERMS_DEV, W, W), BF16)], [any_space], [sems])(right)
    came = lax.ppermute(send, "sector", SWAP)
    (msg,) = call(
        pick_kernel,
        [((pieces, 4 * NBLK, W), BF16)],
        [VMEM, VMEM, SMEM, any_space, any_space],
        [pltpu.VMEM((pieces * 16, W), F32), pltpu.VMEM((pieces * 4 * NBLK, W), F32)],
    )(got, hits, src, came, right)
    got = lax.all_to_all(msg, "sector", 0, 0)
    msg, blk0 = call(
        ham0_kernel,
        [scatter, blocks],
        [SMEM, VMEM, VMEM, VMEM],
        acc,
        flops,
        nbytes,
        limit=16,
    )(dims, got, left, right)
    msg, image0, slab0 = call(reduce0_kernel, [plane, (slab, F32), (slab, F32)], [VMEM] * 3)(
        over_cz(msg), keep, came
    )

    got = over_cz(select(3, over_xy(msg), src))
    msg, blk1, v0, v1, co = call(
        ham1_kernel,
        [scatter, blocks, (slab, F32), (slab, F32), coefs],
        [SMEM] + [VMEM] * 6,
        acc,
        flops,
        nbytes,
        limit=16,
    )(dims, got, left, right, blk0, slab0, image0)
    msg, rest1 = call(reduce1_kernel, [plane, (slab, F32)], [VMEM] * 4)(over_cz(msg), v1, v0, co)

    got = over_cz(select(4, over_xy(msg), src))
    msg, own, v2, co = call(
        ham2_kernel,
        [scatter, ((SEC, W, W), F32), (slab, F32), coefs],
        [SMEM] + [VMEM] * 8,
        [pltpu.VMEM((NBLK, W, W), F32)] + acc,
        flops,
        nbytes,
        limit=16,
    )(dims, got, left, right, blk1, blk0, v1, rest1, co)
    (msg,) = call(reduce2_kernel, [((GRP, SEC * SLAB + 16, W), BF16)], [VMEM] * 4)(
        over_cz(msg), v2, v1, co
    )

    got = over_cz(msg)
    (msg,) = call(sums_kernel, [((CHIPS, 8, W), F32)], [VMEM])(got)
    return call(
        finish_kernel,
        [((SEC, W, W), F32), ((6,), F32), ((SEC, W, W), F32)],
        [VMEM] * 4,
        acc,
        out_specs=[VMEM, SMEM, VMEM],
    )(got, over_xy(msg), own, co)


def solution(mesh):
    placed = (
        P("sector", None, None),
        P("sector", "op", None, None),
        P("sector", "op", None, None),
        P(),
        P("sector", None),
    )
    return jax.shard_map(
        per_device,
        mesh=mesh,
        in_specs=placed,
        out_specs=(P("sector", None, None), P(), P("sector", None, None)),
        check_vma=False,
    )
```

```python
import jax
import jax.numpy as jnp
from jax import lax
from jax.experimental import pallas as pl
from jax.experimental.pallas import tpu as pltpu
from jax.sharding import PartitionSpec as P

F32 = jnp.float32
BF16 = jnp.bfloat16
BOTH = ("sector", "op")
W = 128
SEC = 4
SLAB = 8
NZ = 8
CHIPS = 16
GRP = 16
NBLK = 3 * SEC
WIDE = 2 * NBLK * SLAB
TERMS_DEV = 16
COUNT = float(128 * W * W)
EPS = 1e-06
SCALE = 1.0 / (128.0**0.5)
NCOL = 4

CZ_GROUPS = [[(2 * chip + c) * NZ + z for c in range(2) for z in range(NZ)] for chip in range(CHIPS)]
XY_GROUPS = [[2 * chip + c for chip in range(CHIPS)] for c in range(2)]
SWAP = [(i, i ^ 1) for i in range(2 * CHIPS)]

VMEM = pl.BlockSpec(memory_space=pltpu.VMEM)
SMEM = pl.BlockSpec(memory_space=pltpu.SMEM)


def core_and_z():
    return lax.rem(lax.axis_index("sector"), 2), lax.axis_index("op")


def call(body, outs, specs, scratch=(), flops=0, nbytes=1 << 18, out_specs=None, limit=8):
    return pl.pallas_call(
        body,
        out_shape=[jax.ShapeDtypeStruct(s, d) for s, d in outs],
        in_specs=specs,
        out_specs=out_specs or [VMEM] * len(outs),
        scratch_shapes=list(scratch),
        compiler_params=pltpu.CompilerParams(vmem_limit_bytes=limit << 20),
        cost_estimate=pl.CostEstimate(flops=flops, bytes_accessed=nbytes, transcendentals=0),
    )


def iota(shape, dim):
    return lax.broadcasted_iota(jnp.int32, shape, dim)


def row_sum(x):
    return jnp.sum(x, axis=0, keepdims=True)


def split_rows(rows):
    left_half = iota((1, W), 1) < W // 2
    folded = [row + pltpu.roll(row, W // 2, 1) for row in rows]
    folded += [jnp.zeros((1, W), F32)] * (4 - len(rows))
    return split_again([jnp.where(left_half, folded[2 * k], folded[2 * k + 1]) for k in range(2)])


def split_again(rows):
    at = iota((8, W), 0)
    tile = jnp.zeros((8, W), F32)
    for k, row in enumerate(rows):
        hi = row.astype(BF16).astype(F32)
        mid = (row - hi).astype(BF16).astype(F32)
        low = row - hi - mid
        for n, part in enumerate((hi, mid, low)):
            tile = jnp.where(at == 3 * k + n, jnp.broadcast_to(part, (8, W)), tile)
    return tile.astype(BF16)


def join_rows(tile):
    return [row_sum(tile[3 * k : 3 * k + 3]) for k in range(2)]


def half_totals(rows):
    left_half = iota((1, W), 1) < W // 2
    out = []
    for row in rows:
        out.append(total(jnp.where(left_half, row, 0.0)))
        out.append(total(jnp.where(left_half, 0.0, row)))
    return out


def total(row):
    return jnp.sum(row, axis=1, keepdims=True)


def low_high(low, high):
    first = iota((SLAB, W), 0) < 4
    return (
        jnp.where(first, low, pltpu.roll(high, 4, 0)),
        jnp.where(first, pltpu.roll(low, 4, 0), high),
    )


def start_kernel(theta, dims, msg, keep, send, limits, held, sizes, sems):
    size_copy = pltpu.make_async_copy(dims, sizes, sems.at[SEC])
    copies = [pltpu.make_async_copy(theta.at[i], held.at[i], sems.at[i]) for i in range(SEC)]
    size_copy.start()
    for copy in copies:
        copy.start()
    size_copy.wait()
    at = iota((8, W), 0)
    tile = jnp.zeros((8, W), jnp.int32)
    for i in range(SEC):
        for k in range(2):
            tile = jnp.where(at == 2 * i + k, sizes[k, i], tile)
    limits[...] = tile
    rows = iota((W, W), 0)
    cols = iota((W, W), 1)
    for i in range(SEC):
        copies[i].wait()
        inside = (rows < sizes[0, i]) & (cols < sizes[1, i])
        held[i] = jnp.where(inside, held[i], 0.0)
    for t in range(GRP):
        tiles = [held[i, SLAB * t : SLAB * (t + 1), :] for i in range(SEC)]
        even0, odd0 = low_high(tiles[0], tiles[1])
        even1, odd1 = low_high(tiles[2], tiles[3])
        msg[2 * t] = jnp.concatenate([even0, even1], axis=0).astype(BF16)
        msg[2 * t + 1] = jnp.concatenate([odd0, odd1], axis=0).astype(BF16)
    c, z = core_and_z()
    for slot, out in ((c * NZ + z, keep), ((1 - c) * NZ + z, send)):
        first = pl.multiple_of(slot * SLAB, SLAB)
        for i in range(SEC):
            out[SLAB * i : SLAB * (i + 1), :] = held[i, pl.ds(first, SLAB), :]


def load_kernel(array, held, sems):
    copies = [pltpu.make_async_copy(array.at[i], held.at[i], sems.at[i]) for i in range(SEC)]
    for copy in copies:
        copy.start()
    for copy in copies:
        copy.wait()


def wanted(perm, count, first, shift):
    shape = (count, W)
    row = lax.shift_right_logical(iota(shape, 0), shift)
    at = lax.shift_right_logical(row * 21846, 16)
    q = row - 3 * at
    held = jnp.broadcast_to(perm[...].astype(F32), shape)
    mine = jnp.sum(jnp.where(iota(shape, 1) == at + first, held, 0.0), axis=1, keepdims=True)
    want = mine + q.astype(F32) - 1.0
    want = jnp.where(want < 0.0, want + 128.0, want)
    want = jnp.where(want > 127.0, want - 128.0, want)
    return (held == want).astype(F32).astype(BF16)


def hits_kernel(perm, hits, wide):
    hits[...] = wanted(perm, 3 * W, 0, 0)
    chip = lax.axis_index("sector") // 2
    near = wanted(perm, WIDE, chip * 2 * SEC, 3)
    cols = (W, SLAB * W)
    spread_out = (lax.shift_right_logical(iota(cols, 1), 3) == iota(cols, 0)).astype(F32).astype(BF16)
    both = jnp.dot(near, spread_out, preferred_element_type=F32)
    shape = (WIDE, SLAB * W)
    same = lax.bitwise_and(iota(shape, 0), 7) == lax.bitwise_and(iota(shape, 1), 7)
    wide[...] = jnp.where(same, both, 0.0).astype(BF16)


def pick_kernel(got, hits, came, held, msg, pieces, picked):
    for g in range(2 * CHIPS):
        pieces[16 * g : 16 * (g + 1)] = got[g].astype(F32)
    for r in range(4):
        part = pieces[pl.ds(r, W, stride=4), :].astype(BF16)
        picked[pl.ds(r, 3 * W, stride=4), :] = jnp.dot(hits[...], part, preferred_element_type=F32)
    for g in range(2 * CHIPS):
        msg[g] = picked[48 * g : 48 * (g + 1)].astype(BF16)


def assemble_pieces(got, out):
    for t in range(GRP):
        low = got[2 * t].astype(F32)
        high = got[2 * t + 1].astype(F32)
        for m in range(NBLK // 2):
            at = slice(SLAB * m, SLAB * (m + 1))
            two = low_high(low[at], high[at])
            for k in range(2):
                out[2 * m + k, SLAB * t : SLAB * (t + 1), :] = two[k]


def select_kernel(got, wide, msg):
    data = 2 * SEC * SLAB
    slabs = jnp.concatenate([got[n, :data] for n in range(CHIPS)], axis=0)
    picked = jnp.dot(wide[...], slabs, preferred_element_type=F32).astype(BF16)
    acc = got[0, data:].astype(F32)
    for n in range(1, CHIPS):
        acc = acc + got[n, data:].astype(F32)
    tile = split_again(join_rows(acc))
    for c in range(2):
        half = picked[NBLK * SLAB * c : NBLK * SLAB * (c + 1)]
        for z in range(NZ):
            msg[c * NZ + z, : NBLK * SLAB] = half
            msg[c * NZ + z, NBLK * SLAB :] = tile


def gathered_totals(got):
    acc = got[0, NBLK * SLAB :].astype(F32)
    for s in range(1, GRP):
        acc = acc + got[s, NBLK * SLAB :].astype(F32)
    return half_totals(join_rows(acc))


def assemble(got, out):
    for s in range(GRP):
        for pair in range(NBLK // 2):
            tile = got[s, 16 * pair : 16 * (pair + 1)].astype(F32)
            for k in range(2):
                out[2 * pair + k, SLAB * s : SLAB * (s + 1), :] = tile[SLAB * k : SLAB * (k + 1)]


def products(limits, blocks, left, right, msg, acc):
    _, z = core_and_z()
    rows = iota((W, W), 0)
    cols = iota((W, W), 1)
    for i in range(SEC):
        inner = []
        order = []
        for r in range(3):
            terms = list(range(r, TERMS_DEV, 3))
            vec = blocks[3 * i + lax.rem(z + r, 3)].astype(BF16)
            lhs = jnp.concatenate([left[i, w] for w in terms], axis=0)
            got = jnp.dot(lhs, vec, preferred_element_type=F32).astype(BF16)
            inner += [got[W * n : W * (n + 1)] for n in range(len(terms))]
            order += terms
        lhs = jnp.concatenate(inner, axis=1)
        rhs = jnp.concatenate([right[i, w] for w in order], axis=0)
        out = jnp.dot(lhs, rhs, preferred_element_type=F32)
        inside = (rows < coef(limits, 2 * i)) & (cols < coef(limits, 2 * i + 1))
        acc[i] = jnp.where(inside, out * SCALE, 0.0)
    for s in range(GRP):
        at = slice(SLAB * s, SLAB * (s + 1))
        for pair in range(SEC // 2):
            tile = jnp.concatenate([acc[2 * pair, at, :], acc[2 * pair + 1, at, :]], axis=0)
            msg[s, 16 * pair : 16 * (pair + 1)] = tile.astype(BF16)


def put_coefs(out, values):
    at = iota((8, W), 0)
    tile = jnp.zeros((8, W), F32)
    for k, v in enumerate(values):
        tile = jnp.where(at == k, jnp.broadcast_to(v, (8, W)), tile)
    out[...] = tile


def coef(ref, k):
    return ref[k : k + 1, 0:1]


def ham0_kernel(limits, got, left, right, msg, blk, acc):
    assemble_pieces(got, blk)
    products(limits, blk, left, right, msg, acc)


def ham1_kernel(limits, got, left, right, blk0, slab0, image0, msg, blk, v0, v1, coefs, acc):
    uu, uw, ww, _ = gathered_totals(got)
    assemble(got, blk)
    n2 = uu / COUNT + EPS
    inv = 1.0 / jnp.sqrt(n2)
    a0 = uw / n2 / COUNT
    rr = (ww - 2.0 * a0 * uw + a0 * a0 * uu) / n2
    b1 = jnp.sqrt(jnp.maximum(rr, 0.0) / COUNT + EPS)
    wc = inv / b1
    vc = a0 * wc
    for n in range(NBLK):
        blk[n] = blk[n] * wc - blk0[n] * vc
    v0[...] = slab0[...] * inv
    v1[...] = image0[...] * wc - slab0[...] * vc
    put_coefs(coefs, (a0, b1, inv))
    products(limits, blk, left, right, msg, acc)


def ham2_kernel(
    limits, got, left, right, blk1, blk0, slab1, rest1, old, msg, own, v2, coefs, blk, acc
):
    vw, vr, rr, vv = gathered_totals(got)
    assemble(got, blk)
    a0, b1, inv = coef(old, 0), coef(old, 1), coef(old, 2)
    a1 = vw / COUNT
    d = a1 - a0
    rest = rr - 2.0 * d * vr + d * d * vv
    b2 = jnp.sqrt(jnp.maximum(rest, 0.0) / COUNT + EPS)
    wc = 1.0 / b2
    vc = a1 * wc
    pc = b1 * inv * wc
    for n in range(NBLK):
        blk[n] = blk[n] * wc - blk1[n] * vc - blk0[n] * pc
    for i in range(SEC):
        own[i] = blk[3 * i + 1]
    v2[...] = (rest1[...] - d * slab1[...]) * wc
    put_coefs(coefs, (a0, a1, b1, b2))
    products(limits, blk, left, right, msg, acc)


def reduced(got):
    parts = []
    for c in range(2):
        acc = got[c * NZ].astype(F32)
        for z in range(1, NZ):
            acc = acc + got[c * NZ + z].astype(F32)
        parts.append(acc)
    return jnp.concatenate(parts, axis=0)


def spread(msg, image, rows):
    msg_rows = 2 * SEC * SLAB
    rounded = image.astype(BF16)
    tile = split_rows(rows)
    for n in range(CHIPS):
        msg[n, :msg_rows] = rounded
        msg[n, msg_rows:] = tile


def reduce0_kernel(got, keep, came, msg, image0, slab0):
    c, _ = core_and_z()
    image = reduced(got)
    image0[...] = image
    half = SEC * SLAB
    slab0[:half] = jnp.where(c == 0, keep[...], came[...])
    slab0[half:] = jnp.where(c == 0, came[...], keep[...])
    vec = slab0[...]
    spread(msg, image, [row_sum(vec * vec), row_sum(vec * image), row_sum(image * image)])


def inner_rows(vec, image, rest):
    return [row_sum(vec * image), row_sum(vec * rest), row_sum(rest * rest), row_sum(vec * vec)]


def reduce1_kernel(got, v1, v0, coefs, msg, rest1):
    image = reduced(got)
    vec = v1[...]
    rest = image - coef(coefs, 1) * v0[...] - coef(coefs, 0) * vec
    rest1[...] = rest
    spread(msg, image, inner_rows(vec, image, rest))


def reduce2_kernel(got, v2, v1, coefs, msg):
    image = reduced(got)
    vec = v2[...]
    rest = image - coef(coefs, 3) * v1[...] - coef(coefs, 1) * vec
    half = SEC * SLAB
    tile = split_rows(inner_rows(vec, image, rest))
    for c in range(2):
        rounded = rest[half * c : half * (c + 1)].astype(BF16)
        for z in range(NZ):
            msg[c * NZ + z, :half] = rounded
            msg[c * NZ + z, half:] = tile


def sums_kernel(got, msg):
    half = SEC * SLAB
    acc = got[0, half:].astype(F32)
    for s in range(1, GRP):
        acc = acc + got[s, half:].astype(F32)
    at = iota((8, W), 0)
    tile = jnp.zeros((8, W), F32)
    for k, row in enumerate(join_rows(acc)):
        tile = jnp.where(at == k, jnp.broadcast_to(row, (8, W)), tile)
    for n in range(CHIPS):
        msg[n] = tile


def finish_kernel(got, sums, own, coefs, vec_out, coef_out, dens_out, rest2):
    acc = sums[0]
    for n in range(1, CHIPS):
        acc = acc + sums[n]
    vw, vr, rr, vv = half_totals([acc[k : k + 1] for k in range(2)])
    a0, a1, b1, b2 = [coef(coefs, k) for k in range(4)]
    a2 = vw / COUNT
    d = a2 - a1
    rest = rr - 2.0 * d * vr + d * d * vv
    b3 = jnp.sqrt(jnp.maximum(rest, 0.0) / COUNT + EPS)
    for k, v in enumerate((a0, a1, a2, b1, b2, b3)):
        coef_out[k] = v[0, 0]
    wc = 1.0 / b3
    vc = d * wc
    for s in range(GRP):
        for pair in range(SEC // 2):
            tile = got[s, 16 * pair : 16 * (pair + 1)].astype(F32)
            for k in range(2):
                rest2[2 * pair + k, SLAB * s : SLAB * (s + 1), :] = tile[SLAB * k : SLAB * (k + 1)]
    for i in range(SEC):
        v = rest2[i] * wc - own[i] * vc
        vec_out[i] = v
        dens_out[i] = (
            lax.dot_general(
                v, v, (((1,), (1,)), ((), ())), precision=lax.Precision.HIGHEST, preferred_element_type=F32
            )
            / W
        )


def over_cz(x):
    return lax.all_to_all(x, BOTH, 0, 0, axis_index_groups=CZ_GROUPS)


def over_xy(x):
    return lax.all_to_all(x, "sector", 0, 0, axis_index_groups=XY_GROUPS)


def select(got, wide):
    return call(select_kernel, [((GRP, NBLK * SLAB + 8, W), BF16)], [VMEM, VMEM])(got, wide)[0]


def per_device(theta, left, right, perm, dims):
    half = (SEC * SLAB, W)
    slab = (2 * SEC * SLAB, W)
    scatter = ((GRP, SEC * SLAB, W), BF16)
    plane = ((CHIPS, 2 * SEC * SLAB + 8, W), BF16)
    blocks = ((NBLK, W, W), F32)
    acc = [pltpu.VMEM((SEC, W, W), F32)]
    coefs = ((8, W), F32)
    flops = 2 * 2 * SEC * TERMS_DEV * W**3
    nbytes = 6 << 20

    dims = dims.T
    any_space = pl.BlockSpec(memory_space=pl.ANY)
    pieces = 2 * CHIPS
    sems = pltpu.SemaphoreType.DMA((SEC + 1,))

    msg, keep, send, limits = call(
        start_kernel,
        [((pieces, 16, W), BF16), (half, F32), (half, F32), ((8, W), jnp.int32)],
        [any_space, any_space],
        [pltpu.VMEM((SEC, W, W), F32), pltpu.SMEM((2, SEC), jnp.int32), sems],
        limit=60,
    )(theta, dims)
    got = lax.all_to_all(msg, "sector", 0, 0)
    hits, wide = call(
        hits_kernel, [((3 * W, W), BF16), ((WIDE, SLAB * W), BF16)], [VMEM]
    )(perm.reshape(1, W))
    (right,) = call(load_kernel, [((SEC, TERMS_DEV, W, W), BF16)], [any_space], [sems])(right)
    came = lax.ppermute(send, "sector", SWAP)
    (msg,) = call(
        pick_kernel,
        [((pieces, 4 * NBLK, W), BF16)],
        [VMEM, VMEM, any_space, any_space],
        [pltpu.VMEM((pieces * 16, W), F32), pltpu.VMEM((pieces * 4 * NBLK, W), F32)],
    )(got, hits, came, right)
    got = lax.all_to_all(msg, "sector", 0, 0)
    msg, blk0 = call(
        ham0_kernel,
        [scatter, blocks],
        [VMEM] * 4,
        acc,
        flops,
        nbytes,
        limit=16,
    )(limits, got, left, right)
    msg, image0, slab0 = call(reduce0_kernel, [plane, (slab, F32), (slab, F32)], [VMEM] * 3)(
        over_cz(msg), keep, came
    )

    got = over_cz(select(over_xy(msg), wide))
    msg, blk1, v0, v1, co = call(
        ham1_kernel,
        [scatter, blocks, (slab, F32), (slab, F32), coefs],
        [VMEM] * 7,
        acc,
        flops,
        nbytes,
        limit=16,
    )(limits, got, left, right, blk0, slab0, image0)
    msg, rest1 = call(reduce1_kernel, [plane, (slab, F32)], [VMEM] * 4)(over_cz(msg), v1, v0, co)

    got = over_cz(select(over_xy(msg), wide))
    msg, own, v2, co = call(
        ham2_kernel,
        [scatter, ((SEC, W, W), F32), (slab, F32), coefs],
        [VMEM] * 9,
        [pltpu.VMEM((NBLK, W, W), F32)] + acc,
        flops,
        nbytes,
        limit=16,
    )(limits, got, left, right, blk1, blk0, v1, rest1, co)
    (msg,) = call(reduce2_kernel, [((GRP, SEC * SLAB + 8, W), BF16)], [VMEM] * 4)(
        over_cz(msg), v2, v1, co
    )

    got = over_cz(msg)
    (msg,) = call(sums_kernel, [((CHIPS, 8, W), F32)], [VMEM])(got)
    return call(
        finish_kernel,
        [((SEC, W, W), F32), ((6,), F32), ((SEC, W, W), F32)],
        [VMEM] * 4,
        acc,
        out_specs=[VMEM, SMEM, VMEM],
    )(got, over_xy(msg), own, co)


def solution(mesh):
    placed = (
        P("sector", None, None),
        P("sector", "op", None, None),
        P("sector", "op", None, None),
        P(),
        P("sector", None),
    )
    return jax.shard_map(
        per_device,
        mesh=mesh,
        in_specs=placed,
        out_specs=(P("sector", None, None), P(), P("sector", None, None)),
        check_vma=False,
    )
```

```python
import jax
import jax.numpy as jnp
from jax import lax
from jax.experimental import pallas as pl
from jax.experimental.pallas import tpu as pltpu
from jax.sharding import PartitionSpec as P

F32 = jnp.float32
BF16 = jnp.bfloat16
BOTH = ("sector", "op")
W = 128
SEC = 4
SLAB = 8
NZ = 8
CHIPS = 16
GRP = 16
NBLK = 3 * SEC
HELD = SEC // 2
NEAR = 3 * HELD
WIDE = 2 * NBLK * SLAB
TERMS_DEV = 16
COUNT = float(128 * W * W)
EPS = 1e-06
SCALE = 1.0 / (128.0**0.5)
NCOL = 4

CZ_GROUPS = [[(2 * chip + c) * NZ + z for c in range(2) for z in range(NZ)] for chip in range(CHIPS)]
XY_GROUPS = [[2 * chip + c for chip in range(CHIPS)] for c in range(2)]
SWAP = [(i, i ^ 1) for i in range(2 * CHIPS)]
DOWN = [(i, (i - 1) % NZ) for i in range(NZ)]
UP = [(i, (i + 1) % NZ) for i in range(NZ)]

VMEM = pl.BlockSpec(memory_space=pltpu.VMEM)
SMEM = pl.BlockSpec(memory_space=pltpu.SMEM)


def core_and_z():
    return lax.rem(lax.axis_index("sector"), 2), lax.axis_index("op")


def call(body, outs, specs, scratch=(), flops=0, nbytes=1 << 18, out_specs=None, limit=8):
    return pl.pallas_call(
        body,
        out_shape=[jax.ShapeDtypeStruct(s, d) for s, d in outs],
        in_specs=specs,
        out_specs=out_specs or [VMEM] * len(outs),
        scratch_shapes=list(scratch),
        compiler_params=pltpu.CompilerParams(vmem_limit_bytes=limit << 20),
        cost_estimate=pl.CostEstimate(flops=flops, bytes_accessed=nbytes, transcendentals=0),
    )


def iota(shape, dim):
    return lax.broadcasted_iota(jnp.int32, shape, dim)


def row_sum(x):
    return jnp.sum(x, axis=0, keepdims=True)


def split_rows(rows):
    left_half = iota((1, W), 1) < W // 2
    folded = [row + pltpu.roll(row, W // 2, 1) for row in rows]
    folded += [jnp.zeros((1, W), F32)] * (4 - len(rows))
    return split_again([jnp.where(left_half, folded[2 * k], folded[2 * k + 1]) for k in range(2)])


def split_again(rows):
    at = iota((8, W), 0)
    tile = jnp.zeros((8, W), F32)
    for k, row in enumerate(rows):
        hi = row.astype(BF16).astype(F32)
        mid = (row - hi).astype(BF16).astype(F32)
        low = row - hi - mid
        for n, part in enumerate((hi, mid, low)):
            tile = jnp.where(at == 3 * k + n, jnp.broadcast_to(part, (8, W)), tile)
    return tile.astype(BF16)


def join_rows(tile):
    return [row_sum(tile[3 * k : 3 * k + 3]) for k in range(2)]


def half_totals(rows):
    left_half = iota((1, W), 1) < W // 2
    out = []
    for row in rows:
        out.append(total(jnp.where(left_half, row, 0.0)))
        out.append(total(jnp.where(left_half, 0.0, row)))
    return out


def total(row):
    return jnp.sum(row, axis=1, keepdims=True)


def low_high(low, high):
    first = iota((SLAB, W), 0) < 4
    return (
        jnp.where(first, low, pltpu.roll(high, 4, 0)),
        jnp.where(first, pltpu.roll(low, 4, 0), high),
    )


def start_kernel(
    theta, dims, left, right, msg, keep, send, limits, down, up, held, sizes, stage, sems, out_sems
):
    size_copy = pltpu.make_async_copy(dims, sizes, sems.at[SEC])
    copies = [pltpu.make_async_copy(theta.at[i], held.at[i], sems.at[i]) for i in range(SEC)]
    c, z = core_and_z()
    other = HELD * (1 - lax.rem(z, 2))
    size_copy.start()
    for copy in copies:
        copy.start()
    away = (down, up)
    halves = []
    for m in range(HELD):
        for k, array in enumerate((left, right)):
            halves.append(
                (
                    pltpu.make_async_copy(array.at[other + m], stage.at[m, k], sems.at[SEC + 1 + 2 * m + k]),
                    pltpu.make_async_copy(stage.at[m, k], away[m].at[k], out_sems.at[2 * m + k]),
                )
            )
    for copy, _ in halves:
        copy.start()
    size_copy.wait()
    at = iota((8, W), 0)
    tile = jnp.zeros((8, W), jnp.int32)
    for i in range(SEC):
        for k in range(2):
            tile = jnp.where(at == 2 * i + k, sizes[k, i], tile)
    limits[...] = tile
    rows = iota((W, W), 0)
    cols = iota((W, W), 1)
    for i in range(SEC):
        copies[i].wait()
        if i == SEC - 1:
            for copy, out in halves:
                copy.wait()
                out.start()
        inside = (rows < sizes[0, i]) & (cols < sizes[1, i])
        held[i] = jnp.where(inside, held[i], 0.0)
    for t in range(GRP):
        tiles = [held[i, SLAB * t : SLAB * (t + 1), :] for i in range(SEC)]
        even0, odd0 = low_high(tiles[0], tiles[1])
        even1, odd1 = low_high(tiles[2], tiles[3])
        msg[2 * t] = jnp.concatenate([even0, even1], axis=0).astype(BF16)
        msg[2 * t + 1] = jnp.concatenate([odd0, odd1], axis=0).astype(BF16)
    for slot, out in ((c * NZ + z, keep), ((1 - c) * NZ + z, send)):
        first = pl.multiple_of(slot * SLAB, SLAB)
        for i in range(SEC):
            out[SLAB * i : SLAB * (i + 1), :] = held[i, pl.ds(first, SLAB), :]
    for _, out in halves:
        out.wait()


def wanted(perm, count, first, shift):
    shape = (count, W)
    row = lax.shift_right_logical(iota(shape, 0), shift)
    at = lax.shift_right_logical(row * 21846, 16)
    q = row - 3 * at
    held = jnp.broadcast_to(perm[...].astype(F32), shape)
    mine = jnp.sum(jnp.where(iota(shape, 1) == at + first, held, 0.0), axis=1, keepdims=True)
    want = mine + q.astype(F32) - 1.0
    want = jnp.where(want < 0.0, want + 128.0, want)
    want = jnp.where(want > 127.0, want - 128.0, want)
    return (held == want).astype(F32).astype(BF16)


def hits_kernel(perm, ones):
    hits = wanted(perm, 3 * W, 0, 0)
    part = 3 * W // SLAB
    for k in range(SLAB):
        ones[WIDE:, W * k : W * (k + 1)] = hits[part * k : part * (k + 1)]
    chip = lax.axis_index("sector") // 2
    near = wanted(perm, WIDE, chip * 2 * SEC, 3)
    cols = (W, SLAB * W)
    spread_out = (lax.shift_right_logical(iota(cols, 1), 3) == iota(cols, 0)).astype(F32).astype(BF16)
    both = jnp.dot(near, spread_out, preferred_element_type=F32)
    shape = (WIDE, SLAB * W)
    same = lax.bitwise_and(iota(shape, 0), 7) == lax.bitwise_and(iota(shape, 1), 7)
    ones[:WIDE] = jnp.where(same, both, 0.0).astype(BF16)


def pick_kernel(got, ones, came, held, msg, pieces, picked):
    for g in range(2 * CHIPS):
        pieces[16 * g : 16 * (g + 1)] = got[g].astype(F32)
    hits = jnp.concatenate([ones[WIDE:, W * k : W * (k + 1)] for k in range(SLAB)], axis=0)
    for r in range(4):
        part = pieces[pl.ds(r, W, stride=4), :].astype(BF16)
        picked[pl.ds(r, 3 * W, stride=4), :] = jnp.dot(hits, part, preferred_element_type=F32)
    for g in range(2 * CHIPS):
        msg[g] = picked[48 * g : 48 * (g + 1)].astype(BF16)


def assemble_pieces(got, out):
    for t in range(GRP):
        low = got[2 * t].astype(F32)
        high = got[2 * t + 1].astype(F32)
        for m in range(NBLK // 2):
            at = slice(SLAB * m, SLAB * (m + 1))
            two = low_high(low[at], high[at])
            for k in range(2):
                out[2 * m + k, SLAB * t : SLAB * (t + 1), :] = two[k]


def select_kernel(got, ones, msg):
    data = 2 * SEC * SLAB
    slabs = jnp.concatenate([got[n, :data] for n in range(CHIPS)], axis=0)
    picked = jnp.dot(ones[:WIDE], slabs, preferred_element_type=F32).astype(BF16)
    acc = got[0, data:].astype(F32)
    for n in range(1, CHIPS):
        acc = acc + got[n, data:].astype(F32)
    tile = split_again(join_rows(acc))
    rows = NEAR * SLAB
    for c in range(2):
        for z in range(NZ):
            first = rows * (2 * c + z % 2)
            msg[c * NZ + z, :rows] = picked[first : first + rows]
            msg[c * NZ + z, rows:] = tile


def summed_tile(got, first):
    acc = got[0, first:].astype(F32)
    for s in range(1, GRP):
        acc = acc + got[s, first:].astype(F32)
    return join_rows(acc)


def assemble(got, out):
    for s in range(GRP):
        for pair in range(NEAR // 2):
            tile = got[s, 16 * pair : 16 * (pair + 1)].astype(F32)
            for k in range(2):
                out[2 * pair + k, SLAB * s : SLAB * (s + 1), :] = tile[SLAB * k : SLAB * (k + 1)]


def products(limits, blocks, left, right, msg, acc):
    _, z = core_and_z()
    rows = iota((W, W), 0)
    cols = iota((W, W), 1)
    for i in range(SEC):
        inner = []
        order = []
        for r in range(3):
            terms = list(range(r, TERMS_DEV, 3))
            vec = blocks[3 * i + lax.rem(z + r, 3)].astype(BF16)
            lhs = jnp.concatenate([left[i, w] for w in terms], axis=0)
            got = jnp.dot(lhs, vec, preferred_element_type=F32).astype(BF16)
            inner += [got[W * n : W * (n + 1)] for n in range(len(terms))]
            order += terms
        lhs = jnp.concatenate(inner, axis=1)
        rhs = jnp.concatenate([right[i, w] for w in order], axis=0)
        out = jnp.dot(lhs, rhs, preferred_element_type=F32)
        inside = (rows < coef(limits, 2 * i)) & (cols < coef(limits, 2 * i + 1))
        acc[i] = jnp.where(inside, out * SCALE, 0.0)
    for s in range(GRP):
        at = slice(SLAB * s, SLAB * (s + 1))
        for pair in range(SEC // 2):
            tile = jnp.concatenate([acc[2 * pair, at, :], acc[2 * pair + 1, at, :]], axis=0)
            msg[s, 16 * pair : 16 * (pair + 1)] = tile.astype(BF16)


def start_copies(above, below, near, sems):
    copies = []
    for m, array in enumerate((above, below)):
        for k in range(2):
            copy = pltpu.make_async_copy(array.at[k], near.at[m, k], sems.at[2 * m + k])
            copy.start()
            copies.append(copy)
    return copies


def products_held(limits, blocks, left, right, extra, msg, acc):
    _, z = core_and_z()
    odd = lax.rem(z, 2)
    rows = iota((W, W), 0)
    cols = iota((W, W), 1)
    inner = [[], []]
    rhs = [[], []]
    for mine in (True, False):
        for m in range(HELD):
            i = HELD * odd + m
            start = z if mine else lax.rem(z + (NZ + 1 - 2 * m), NZ)
            for r in range(3):
                terms = range(r, TERMS_DEV, 3)
                vec = blocks[3 * m + lax.rem(start + r, 3)].astype(BF16)
                lhs = jnp.concatenate([left[i, w] if mine else extra[m, 0, w] for w in terms], axis=0)
                got = jnp.dot(lhs, vec, preferred_element_type=F32).astype(BF16)
                inner[m] += [got[W * n : W * (n + 1)] for n in range(len(terms))]
                rhs[m] += [right[i, w] if mine else extra[m, 1, w] for w in terms]
    for m in range(HELD):
        i = HELD * odd + m
        lhs = jnp.concatenate(inner[m], axis=1)
        out = jnp.dot(lhs, jnp.concatenate(rhs[m], axis=0), preferred_element_type=F32)
        size = limits[pl.ds(2 * i, 1), 0:1], limits[pl.ds(2 * i + 1, 1), 0:1]
        acc[m] = jnp.where((rows < size[0]) & (cols < size[1]), out * SCALE, 0.0)
    for s in range(GRP):
        at = slice(SLAB * s, SLAB * (s + 1))
        msg[s, :16] = jnp.concatenate([acc[0, at, :], acc[1, at, :]], axis=0).astype(BF16)


def put_coefs(out, values):
    at = iota((8, W), 0)
    tile = jnp.zeros((8, W), F32)
    for k, v in enumerate(values):
        tile = jnp.where(at == k, jnp.broadcast_to(v, (8, W)), tile)
    out[...] = tile


def coef(ref, k):
    return ref[k : k + 1, 0:1]


def ham0_kernel(limits, got, left, right, above, below, msg, blk, near, acc, sems):
    copies = start_copies(above, below, near, sems)
    assemble_pieces(got, blk)
    products(limits, blk, left, right, msg, acc)
    for copy in copies:
        copy.wait()


def ham1_kernel(
    limits, got, left, right, near, blk0, slab0, image0, msg, blk, v0, v1, coefs, acc
):
    first = NEAR * lax.rem(core_and_z()[1], 2)
    uu, uw, ww, _ = half_totals(summed_tile(got, NEAR * SLAB))
    assemble(got, blk)
    n2 = uu / COUNT + EPS
    inv = 1.0 / jnp.sqrt(n2)
    a0 = uw / n2 / COUNT
    rr = (ww - 2.0 * a0 * uw + a0 * a0 * uu) / n2
    b1 = jnp.sqrt(jnp.maximum(rr, 0.0) / COUNT + EPS)
    wc = inv / b1
    vc = a0 * wc
    for n in range(NEAR):
        blk[n] = blk[n] * wc - blk0[first + n] * vc
    v0[...] = slab0[...] * inv
    v1[...] = image0[...] * wc - slab0[...] * vc
    put_coefs(coefs, (a0, b1, inv))
    products_held(limits, blk, left, right, near, msg, acc)


def ham2_kernel(
    limits, got, left, right, near, blk1, blk0, slab1, rest1, old, msg, v2, coefs, blk, acc
):
    first = NEAR * lax.rem(core_and_z()[1], 2)
    vw, vr, rr, vv = half_totals(summed_tile(got, NEAR * SLAB))
    assemble(got, blk)
    a0, b1, inv = coef(old, 0), coef(old, 1), coef(old, 2)
    a1 = vw / COUNT
    d = a1 - a0
    rest = rr - 2.0 * d * vr + d * d * vv
    b2 = jnp.sqrt(jnp.maximum(rest, 0.0) / COUNT + EPS)
    wc = 1.0 / b2
    vc = a1 * wc
    pc = b1 * inv * wc
    for n in range(NEAR):
        blk[n] = blk[n] * wc - blk1[n] * vc - blk0[first + n] * pc
    v2[...] = (rest1[...] - d * slab1[...]) * wc
    put_coefs(coefs, (a0, a1, b1, b2))
    products_held(limits, blk, left, right, near, msg, acc)
    dots = row_sum(sum(blk[3 * m + 1] * acc[m] for m in range(HELD)))
    tile = split_rows([dots])
    for s in range(GRP):
        msg[s, 16:] = tile


def reduced(got):
    parts = []
    for c in range(2):
        acc = got[c * NZ].astype(F32)
        for z in range(1, NZ):
            acc = acc + got[c * NZ + z].astype(F32)
        parts.append(acc)
    return jnp.concatenate(parts, axis=0)


def reduced_halves(got):
    parts = []
    for c in range(2):
        for odd in range(2):
            acc = got[c * NZ + odd, :16].astype(F32)
            for z in range(odd + 2, NZ, 2):
                acc = acc + got[c * NZ + z, :16].astype(F32)
            parts.append(acc)
    return jnp.concatenate(parts, axis=0)


def spread(msg, image, rows):
    msg_rows = 2 * SEC * SLAB
    rounded = image.astype(BF16)
    tile = split_rows(rows)
    for n in range(CHIPS):
        msg[n, :msg_rows] = rounded
        msg[n, msg_rows:] = tile


def reduce0_kernel(got, keep, came, msg, image0, slab0):
    c, _ = core_and_z()
    image = reduced(got)
    image0[...] = image
    half = SEC * SLAB
    slab0[:half] = jnp.where(c == 0, keep[...], came[...])
    slab0[half:] = jnp.where(c == 0, came[...], keep[...])
    vec = slab0[...]
    spread(msg, image, [row_sum(vec * vec), row_sum(vec * image), row_sum(image * image)])


def inner_rows(vec, image, rest):
    return [row_sum(vec * image), row_sum(vec * rest), row_sum(rest * rest), row_sum(vec * vec)]


def reduce1_kernel(got, v1, v0, coefs, msg, rest1):
    image = reduced_halves(got)
    vec = v1[...]
    rest = image - coef(coefs, 1) * v0[...] - coef(coefs, 0) * vec
    rest1[...] = rest
    spread(msg, image, inner_rows(vec, image, rest))


def reduce2_kernel(got, v2, v1, coefs, msg, rest2):
    image = reduced_halves(got)
    vec = v2[...]
    rest = image - coef(coefs, 3) * v1[...] - coef(coefs, 1) * vec
    rest2[...] = rest
    rows = [summed_tile(got, 16)[0]] + inner_rows(vec, image, rest)[1:]
    at = iota((8, W), 0)
    tile = jnp.zeros((8, W), F32)
    for k, row in enumerate(rows):
        tile = jnp.where(at == k, jnp.broadcast_to(row, (8, W)), tile)
    for n in range(CHIPS):
        msg[n] = tile


def residual_kernel(got, rest2, v2, coefs, msg, last):
    acc = got[0]
    for n in range(1, CHIPS):
        acc = acc + got[n]
    a2 = total(acc[0:1]) / COUNT
    d = a2 - coef(coefs, 1)
    put_coefs(last, (a2, d))
    rounded = (rest2[...] - d * v2[...]).astype(BF16)
    tile = split_rows([acc[k : k + 1] for k in range(1, 4)])
    half = SEC * SLAB
    for c in range(2):
        for z in range(NZ):
            msg[c * NZ + z, :half] = rounded[half * c : half * (c + 1)]
            msg[c * NZ + z, half:] = tile


def finish_kernel(got, coefs, last, vec_out, coef_out, dens_out, rest):
    vr, rr, vv, _ = half_totals(summed_tile(got, SEC * SLAB))
    a0, a1, b1, b2 = [coef(coefs, k) for k in range(4)]
    a2, d = coef(last, 0), coef(last, 1)
    norm = rr - 2.0 * d * vr + d * d * vv
    b3 = jnp.sqrt(jnp.maximum(norm, 0.0) / COUNT + EPS)
    for k, v in enumerate((a0, a1, a2, b1, b2, b3)):
        coef_out[k] = v[0, 0]
    wc = 1.0 / b3
    for s in range(GRP):
        for pair in range(SEC // 2):
            tile = got[s, 16 * pair : 16 * (pair + 1)].astype(F32)
            for k in range(2):
                rest[2 * pair + k, SLAB * s : SLAB * (s + 1), :] = tile[SLAB * k : SLAB * (k + 1)]
    for i in range(SEC):
        v = rest[i] * wc
        vec_out[i] = v
        dens_out[i] = (
            lax.dot_general(
                v, v, (((1,), (1,)), ((), ())), precision=lax.Precision.HIGHEST, preferred_element_type=F32
            )
            / W
        )


def over_cz(x):
    return lax.all_to_all(x, BOTH, 0, 0, axis_index_groups=CZ_GROUPS)


def over_xy(x):
    return lax.all_to_all(x, "sector", 0, 0, axis_index_groups=XY_GROUPS)


def select(got, ones):
    return call(select_kernel, [((GRP, NEAR * SLAB + 8, W), BF16)], [VMEM, VMEM])(got, ones)[0]


def per_device(theta, left, right, perm, dims):
    half = (SEC * SLAB, W)
    slab = (2 * SEC * SLAB, W)
    scatter = ((GRP, SEC * SLAB, W), BF16)
    plane = ((CHIPS, 2 * SEC * SLAB + 8, W), BF16)
    blocks = ((NBLK, W, W), F32)
    acc = [pltpu.VMEM((SEC, W, W), F32)]
    coefs = ((8, W), F32)
    flops = 2 * 2 * SEC * TERMS_DEV * W**3
    nbytes = 6 << 20

    dims = dims.T
    any_space = pl.BlockSpec(memory_space=pl.ANY)
    pieces = 2 * CHIPS
    away_type = ((2, TERMS_DEV, W, W), BF16)
    near_type = ((HELD, 2, TERMS_DEV, W, W), BF16)
    sems = pltpu.SemaphoreType.DMA((SEC + 1 + 2 * HELD,))

    msg, keep, send, limits, down, up = call(
        start_kernel,
        [((pieces, 16, W), BF16), (half, F32), (half, F32), ((8, W), jnp.int32), away_type, away_type],
        [any_space] * 4,
        [
            pltpu.VMEM((SEC, W, W), F32),
            pltpu.SMEM((2, SEC), jnp.int32),
            pltpu.VMEM(*near_type),
            sems,
            pltpu.SemaphoreType.DMA((2 * HELD,)),
        ],
        out_specs=[VMEM] * 4 + [any_space] * 2,
        limit=60,
    )(theta, dims, left, right)
    above = lax.ppermute(down, "op", DOWN)
    below = lax.ppermute(up, "op", UP)
    got = lax.all_to_all(msg, "sector", 0, 0)
    (ones,) = call(hits_kernel, [((WIDE + 3 * W // SLAB, SLAB * W), BF16)], [VMEM])(perm.reshape(1, W))
    came = lax.ppermute(send, "sector", SWAP)
    (msg,) = call(
        pick_kernel,
        [((pieces, 4 * NBLK, W), BF16)],
        [VMEM, VMEM, any_space, any_space],
        [pltpu.VMEM((pieces * 16, W), F32), pltpu.VMEM((pieces * 4 * NBLK, W), F32)],
    )(got, ones, came, right)
    got = lax.all_to_all(msg, "sector", 0, 0)
    msg, blk0, near = call(
        ham0_kernel,
        [scatter, blocks, near_type],
        [VMEM] * 4 + [any_space] * 2,
        acc + [pltpu.SemaphoreType.DMA((2 * HELD,))],
        flops,
        nbytes,
        limit=20,
    )(limits, got, left, right, above, below)
    msg, image0, slab0 = call(reduce0_kernel, [plane, (slab, F32), (slab, F32)], [VMEM] * 3)(
        over_cz(msg), keep, came
    )

    held = ((NEAR, W, W), F32)
    acc = [pltpu.VMEM((HELD, W, W), F32)]
    got = over_cz(select(over_xy(msg), ones))
    msg, blk1, v0, v1, co = call(
        ham1_kernel,
        [((GRP, 16, W), BF16), held, (slab, F32), (slab, F32), coefs],
        [VMEM] * 8,
        acc,
        flops,
        nbytes,
        limit=20,
    )(limits, got, left, right, near, blk0, slab0, image0)
    msg, rest1 = call(reduce1_kernel, [plane, (slab, F32)], [VMEM] * 4)(over_cz(msg), v1, v0, co)

    got = over_cz(select(over_xy(msg), ones))
    msg, v2, co = call(
        ham2_kernel,
        [((GRP, 24, W), BF16), (slab, F32), coefs],
        [VMEM] * 10,
        [pltpu.VMEM((NEAR, W, W), F32)] + acc,
        flops,
        nbytes,
        limit=20,
    )(limits, got, left, right, near, blk1, blk0, v1, rest1, co)
    msg, rest2 = call(reduce2_kernel, [((CHIPS, 8, W), F32), (slab, F32)], [VMEM] * 4)(
        over_cz(msg), v2, v1, co
    )

    msg, last = call(residual_kernel, [((GRP, SEC * SLAB + 8, W), BF16), coefs], [VMEM] * 4)(
        over_xy(msg), rest2, v2, co
    )
    return call(
        finish_kernel,
        [((SEC, W, W), F32), ((6,), F32), ((SEC, W, W), F32)],
        [VMEM] * 3,
        [pltpu.VMEM((SEC, W, W), F32)],
        out_specs=[VMEM, SMEM, VMEM],
    )(over_cz(msg), co, last)


def solution(mesh):
    placed = (
        P("sector", None, None),
        P("sector", "op", None, None),
        P("sector", "op", None, None),
        P(),
        P("sector", None),
    )
    return jax.shard_map(
        per_device,
        mesh=mesh,
        in_specs=placed,
        out_specs=(P("sector", None, None), P(), P("sector", None, None)),
        check_vma=False,
    )
```

```python
import jax
import jax.numpy as jnp
from jax import lax
from jax.experimental import pallas as pl
from jax.experimental.pallas import tpu as pltpu
from jax.sharding import PartitionSpec as P

F32 = jnp.float32
BF16 = jnp.bfloat16
BOTH = ("sector", "op")
W = 128
SEC = 4
SLAB = 8
NZ = 8
CHIPS = 16
GRP = 16
NBLK = 3 * SEC
HELD = SEC // 2
NEAR = 3 * HELD
WIDE = 2 * NBLK * SLAB
TERMS_DEV = 16
COUNT = float(128 * W * W)
EPS = 1e-06
SCALE = 1.0 / (128.0**0.5)
NCOL = 4

CZ_GROUPS = [[(2 * chip + c) * NZ + z for c in range(2) for z in range(NZ)] for chip in range(CHIPS)]
XY_GROUPS = [[2 * chip + c for chip in range(CHIPS)] for c in range(2)]
SWAP = [(i, i ^ 1) for i in range(2 * CHIPS)]
DOWN = [(i, (i - 1) % NZ) for i in range(NZ)]
UP = [(i, (i + 1) % NZ) for i in range(NZ)]

VMEM = pl.BlockSpec(memory_space=pltpu.VMEM)
SMEM = pl.BlockSpec(memory_space=pltpu.SMEM)


def core_and_z():
    return lax.rem(lax.axis_index("sector"), 2), lax.axis_index("op")


def call(body, outs, specs, scratch=(), flops=0, nbytes=1 << 18, out_specs=None, limit=8):
    return pl.pallas_call(
        body,
        out_shape=[jax.ShapeDtypeStruct(s, d) for s, d in outs],
        in_specs=specs,
        out_specs=out_specs or [VMEM] * len(outs),
        scratch_shapes=list(scratch),
        compiler_params=pltpu.CompilerParams(vmem_limit_bytes=limit << 20),
        cost_estimate=pl.CostEstimate(flops=flops, bytes_accessed=nbytes, transcendentals=0),
    )


def iota(shape, dim):
    return lax.broadcasted_iota(jnp.int32, shape, dim)


def row_sum(x):
    return jnp.sum(x, axis=0, keepdims=True)


def split_rows(rows):
    left_half = iota((1, W), 1) < W // 2
    folded = [row + pltpu.roll(row, W // 2, 1) for row in rows]
    folded += [jnp.zeros((1, W), F32)] * (4 - len(rows))
    return split_again([jnp.where(left_half, folded[2 * k], folded[2 * k + 1]) for k in range(2)])


def split_again(rows):
    at = iota((8, W), 0)
    tile = jnp.zeros((8, W), F32)
    for k, row in enumerate(rows):
        hi = row.astype(BF16).astype(F32)
        mid = (row - hi).astype(BF16).astype(F32)
        low = row - hi - mid
        for n, part in enumerate((hi, mid, low)):
            tile = jnp.where(at == 3 * k + n, jnp.broadcast_to(part, (8, W)), tile)
    return tile.astype(BF16)


def join_rows(tile):
    return [row_sum(tile[3 * k : 3 * k + 3]) for k in range(2)]


def half_totals(rows):
    left_half = iota((1, W), 1) < W // 2
    out = []
    for row in rows:
        out.append(total(jnp.where(left_half, row, 0.0)))
        out.append(total(jnp.where(left_half, 0.0, row)))
    return out


def total(row):
    return jnp.sum(row, axis=1, keepdims=True)


def low_high(low, high):
    first = iota((SLAB, W), 0) < 4
    return (
        jnp.where(first, low, pltpu.roll(high, 4, 0)),
        jnp.where(first, pltpu.roll(low, 4, 0), high),
    )


def start_kernel(
    theta, dims, left, right, msg, keep, send, limits, down, up, held, sizes, stage, sems, out_sems
):
    size_copy = pltpu.make_async_copy(dims, sizes, sems.at[SEC])
    copies = [pltpu.make_async_copy(theta.at[i], held.at[i], sems.at[i]) for i in range(SEC)]
    c, z = core_and_z()
    other = HELD * (1 - lax.rem(z, 2))
    size_copy.start()
    for copy in copies:
        copy.start()
    away = (down, up)
    halves = []
    for m in range(HELD):
        for k, array in enumerate((left, right)):
            halves.append(
                (
                    pltpu.make_async_copy(array.at[other + m], stage.at[m, k], sems.at[SEC + 1 + 2 * m + k]),
                    pltpu.make_async_copy(stage.at[m, k], away[m].at[k], out_sems.at[2 * m + k]),
                )
            )
    for copy, _ in halves:
        copy.start()
    size_copy.wait()
    at = iota((8, W), 0)
    tile = jnp.zeros((8, W), jnp.int32)
    for i in range(SEC):
        for k in range(2):
            tile = jnp.where(at == 2 * i + k, sizes[k, i], tile)
    limits[...] = tile
    rows = iota((W, W), 0)
    cols = iota((W, W), 1)
    for i in range(SEC):
        copies[i].wait()
        if i == SEC - 1:
            for copy, out in halves:
                copy.wait()
                out.start()
        inside = (rows < sizes[0, i]) & (cols < sizes[1, i])
        held[i] = jnp.where(inside, held[i], 0.0)
    for t in range(GRP):
        tiles = [held[i, SLAB * t : SLAB * (t + 1), :] for i in range(SEC)]
        even0, odd0 = low_high(tiles[0], tiles[1])
        even1, odd1 = low_high(tiles[2], tiles[3])
        msg[2 * t] = jnp.concatenate([even0, even1], axis=0).astype(BF16)
        msg[2 * t + 1] = jnp.concatenate([odd0, odd1], axis=0).astype(BF16)
    for slot, out in ((c * NZ + z, keep), ((1 - c) * NZ + z, send)):
        first = pl.multiple_of(slot * SLAB, SLAB)
        for i in range(SEC):
            out[SLAB * i : SLAB * (i + 1), :] = held[i, pl.ds(first, SLAB), :]
    for _, out in halves:
        out.wait()


def wanted(perm, count, first, shift, sides):
    shape = (count, W)
    row = lax.shift_right_logical(iota(shape, 0), shift)
    if sides:
        at = lax.shift_right_logical(row, 1)
        q = 2 * lax.bitwise_and(row, 1)
    else:
        at = lax.shift_right_logical(row * 21846, 16)
        q = row - 3 * at
    held = jnp.broadcast_to(perm[...].astype(F32), shape)
    mine = jnp.sum(jnp.where(iota(shape, 1) == at + first, held, 0.0), axis=1, keepdims=True)
    want = mine + q.astype(F32) - 1.0
    want = jnp.where(want < 0.0, want + 128.0, want)
    want = jnp.where(want > 127.0, want - 128.0, want)
    return (held == want).astype(F32).astype(BF16)


def hits_kernel(perm, ones):
    hits = wanted(perm, 2 * W, 0, 0, True)
    part = 2 * W // SLAB
    for k in range(SLAB):
        ones[WIDE:, W * k : W * (k + 1)] = hits[part * k : part * (k + 1)]
    chip = lax.axis_index("sector") // 2
    near = wanted(perm, WIDE, chip * 2 * SEC, 3, False)
    cols = (W, SLAB * W)
    spread_out = (lax.shift_right_logical(iota(cols, 1), 3) == iota(cols, 0)).astype(F32).astype(BF16)
    both = jnp.dot(near, spread_out, preferred_element_type=F32)
    shape = (WIDE, SLAB * W)
    same = lax.bitwise_and(iota(shape, 0), 7) == lax.bitwise_and(iota(shape, 1), 7)
    ones[:WIDE] = jnp.where(same, both, 0.0).astype(BF16)


def pick_kernel(got, ones, came, held, msg, pieces, picked):
    for g in range(2 * CHIPS):
        pieces[16 * g : 16 * (g + 1)] = got[g].astype(F32)
    hits = jnp.concatenate([ones[WIDE:, W * k : W * (k + 1)] for k in range(SLAB)], axis=0)
    for r in range(4):
        part = pieces[pl.ds(r, W, stride=4), :].astype(BF16)
        picked[pl.ds(r, 2 * W, stride=4), :] = jnp.dot(hits, part, preferred_element_type=F32)
    for g in range(2 * CHIPS):
        msg[g] = picked[32 * g : 32 * (g + 1)].astype(BF16)


def assemble_pieces(got, theta, limits, out):
    for t in range(GRP):
        low = got[2 * t].astype(F32)
        high = got[2 * t + 1].astype(F32)
        for i in range(SEC):
            at = slice(SLAB * i, SLAB * (i + 1))
            two = low_high(low[at], high[at])
            for k in range(2):
                out[3 * i + 2 * k, SLAB * t : SLAB * (t + 1), :] = two[k]
    rows = iota((W, W), 0)
    cols = iota((W, W), 1)
    for i in range(SEC):
        inside = (rows < coef(limits, 2 * i)) & (cols < coef(limits, 2 * i + 1))
        out[3 * i + 1] = jnp.where(inside, theta[i], 0.0)


def select_kernel(got, ones, msg):
    data = 2 * SEC * SLAB
    slabs = jnp.concatenate([got[n, :data] for n in range(CHIPS)], axis=0)
    picked = jnp.dot(ones[:WIDE], slabs, preferred_element_type=F32).astype(BF16)
    acc = got[0, data:].astype(F32)
    for n in range(1, CHIPS):
        acc = acc + got[n, data:].astype(F32)
    tile = split_again(join_rows(acc))
    rows = NEAR * SLAB
    for c in range(2):
        for z in range(NZ):
            first = rows * (2 * c + z % 2)
            msg[c * NZ + z, :rows] = picked[first : first + rows]
            msg[c * NZ + z, rows:] = tile


def summed_tile(got, first):
    acc = got[0, first:].astype(F32)
    for s in range(1, GRP):
        acc = acc + got[s, first:].astype(F32)
    return join_rows(acc)


def assemble(got, out):
    for s in range(GRP):
        for pair in range(NEAR // 2):
            tile = got[s, 16 * pair : 16 * (pair + 1)].astype(F32)
            for k in range(2):
                out[2 * pair + k, SLAB * s : SLAB * (s + 1), :] = tile[SLAB * k : SLAB * (k + 1)]


def products(limits, blocks, left, right, msg, acc):
    _, z = core_and_z()
    rows = iota((W, W), 0)
    cols = iota((W, W), 1)
    for i in range(SEC):
        inner = []
        order = []
        for r in range(3):
            terms = list(range(r, TERMS_DEV, 3))
            vec = blocks[3 * i + lax.rem(z + r, 3)].astype(BF16)
            lhs = jnp.concatenate([left[i, w] for w in terms], axis=0)
            got = jnp.dot(lhs, vec, preferred_element_type=F32).astype(BF16)
            inner += [got[W * n : W * (n + 1)] for n in range(len(terms))]
            order += terms
        lhs = jnp.concatenate(inner, axis=1)
        rhs = jnp.concatenate([right[i, w] for w in order], axis=0)
        out = jnp.dot(lhs, rhs, preferred_element_type=F32)
        inside = (rows < coef(limits, 2 * i)) & (cols < coef(limits, 2 * i + 1))
        acc[i] = jnp.where(inside, out * SCALE, 0.0)
    for s in range(GRP):
        at = slice(SLAB * s, SLAB * (s + 1))
        for pair in range(SEC // 2):
            tile = jnp.concatenate([acc[2 * pair, at, :], acc[2 * pair + 1, at, :]], axis=0)
            msg[s, 16 * pair : 16 * (pair + 1)] = tile.astype(BF16)


def start_copies(above, below, near, sems):
    copies = []
    for m, array in enumerate((above, below)):
        for k in range(2):
            copy = pltpu.make_async_copy(array.at[k], near.at[m, k], sems.at[2 * m + k])
            copy.start()
            copies.append(copy)
    return copies


def products_held(limits, blocks, left, right, extra, msg, acc):
    _, z = core_and_z()
    odd = lax.rem(z, 2)
    rows = iota((W, W), 0)
    cols = iota((W, W), 1)
    inner = [[], []]
    rhs = [[], []]
    for mine in (True, False):
        for m in range(HELD):
            i = HELD * odd + m
            start = z if mine else lax.rem(z + (NZ + 1 - 2 * m), NZ)
            for r in range(3):
                terms = range(r, TERMS_DEV, 3)
                vec = blocks[3 * m + lax.rem(start + r, 3)].astype(BF16)
                lhs = jnp.concatenate([left[i, w] if mine else extra[m, 0, w] for w in terms], axis=0)
                got = jnp.dot(lhs, vec, preferred_element_type=F32).astype(BF16)
                inner[m] += [got[W * n : W * (n + 1)] for n in range(len(terms))]
                rhs[m] += [right[i, w] if mine else extra[m, 1, w] for w in terms]
    for m in range(HELD):
        i = HELD * odd + m
        lhs = jnp.concatenate(inner[m], axis=1)
        out = jnp.dot(lhs, jnp.concatenate(rhs[m], axis=0), preferred_element_type=F32)
        size = limits[pl.ds(2 * i, 1), 0:1], limits[pl.ds(2 * i + 1, 1), 0:1]
        acc[m] = jnp.where((rows < size[0]) & (cols < size[1]), out * SCALE, 0.0)
    for s in range(GRP):
        at = slice(SLAB * s, SLAB * (s + 1))
        msg[s, :16] = jnp.concatenate([acc[0, at, :], acc[1, at, :]], axis=0).astype(BF16)


def put_coefs(out, values):
    at = iota((8, W), 0)
    tile = jnp.zeros((8, W), F32)
    for k, v in enumerate(values):
        tile = jnp.where(at == k, jnp.broadcast_to(v, (8, W)), tile)
    out[...] = tile


def coef(ref, k):
    return ref[k : k + 1, 0:1]


def ham0_kernel(limits, theta, got, left, right, above, below, msg, blk, near, acc, sems):
    copies = start_copies(above, below, near, sems)
    assemble_pieces(got, theta, limits, blk)
    products(limits, blk, left, right, msg, acc)
    for copy in copies:
        copy.wait()


def ham1_kernel(
    limits, got, left, right, near, blk0, slab0, image0, msg, blk, v0, v1, coefs, acc
):
    first = NEAR * lax.rem(core_and_z()[1], 2)
    uu, uw, ww, _ = half_totals(summed_tile(got, NEAR * SLAB))
    assemble(got, blk)
    n2 = uu / COUNT + EPS
    inv = 1.0 / jnp.sqrt(n2)
    a0 = uw / n2 / COUNT
    rr = (ww - 2.0 * a0 * uw + a0 * a0 * uu) / n2
    b1 = jnp.sqrt(jnp.maximum(rr, 0.0) / COUNT + EPS)
    wc = inv / b1
    vc = a0 * wc
    for n in range(NEAR):
        blk[n] = blk[n] * wc - blk0[first + n] * vc
    v0[...] = slab0[...] * inv
    v1[...] = image0[...] * wc - slab0[...] * vc
    put_coefs(coefs, (a0, b1, inv))
    products_held(limits, blk, left, right, near, msg, acc)


def ham2_kernel(
    limits, got, left, right, near, blk1, blk0, slab1, rest1, old, msg, v2, coefs, blk, acc
):
    first = NEAR * lax.rem(core_and_z()[1], 2)
    vw, vr, rr, vv = half_totals(summed_tile(got, NEAR * SLAB))
    assemble(got, blk)
    a0, b1, inv = coef(old, 0), coef(old, 1), coef(old, 2)
    a1 = vw / COUNT
    d = a1 - a0
    rest = rr - 2.0 * d * vr + d * d * vv
    b2 = jnp.sqrt(jnp.maximum(rest, 0.0) / COUNT + EPS)
    wc = 1.0 / b2
    vc = a1 * wc
    pc = b1 * inv * wc
    for n in range(NEAR):
        blk[n] = blk[n] * wc - blk1[n] * vc - blk0[first + n] * pc
    v2[...] = (rest1[...] - d * slab1[...]) * wc
    put_coefs(coefs, (a0, a1, b1, b2))
    products_held(limits, blk, left, right, near, msg, acc)
    dots = row_sum(sum(blk[3 * m + 1] * acc[m] for m in range(HELD)))
    tile = split_rows([dots])
    for s in range(GRP):
        msg[s, 16:] = tile


def reduced(got):
    parts = []
    for c in range(2):
        acc = got[c * NZ].astype(F32)
        for z in range(1, NZ):
            acc = acc + got[c * NZ + z].astype(F32)
        parts.append(acc)
    return jnp.concatenate(parts, axis=0)


def reduced_halves(got):
    parts = []
    for c in range(2):
        for odd in range(2):
            acc = got[c * NZ + odd, :16].astype(F32)
            for z in range(odd + 2, NZ, 2):
                acc = acc + got[c * NZ + z, :16].astype(F32)
            parts.append(acc)
    return jnp.concatenate(parts, axis=0)


def spread(msg, image, rows):
    msg_rows = 2 * SEC * SLAB
    rounded = image.astype(BF16)
    tile = split_rows(rows)
    for n in range(CHIPS):
        msg[n, :msg_rows] = rounded
        msg[n, msg_rows:] = tile


def reduce0_kernel(got, keep, came, msg, image0, slab0):
    c, _ = core_and_z()
    image = reduced(got)
    image0[...] = image
    half = SEC * SLAB
    slab0[:half] = jnp.where(c == 0, keep[...], came[...])
    slab0[half:] = jnp.where(c == 0, came[...], keep[...])
    vec = slab0[...]
    spread(msg, image, [row_sum(vec * vec), row_sum(vec * image), row_sum(image * image)])


def inner_rows(vec, image, rest):
    return [row_sum(vec * image), row_sum(vec * rest), row_sum(rest * rest), row_sum(vec * vec)]


def reduce1_kernel(got, v1, v0, coefs, msg, rest1):
    image = reduced_halves(got)
    vec = v1[...]
    rest = image - coef(coefs, 1) * v0[...] - coef(coefs, 0) * vec
    rest1[...] = rest
    spread(msg, image, inner_rows(vec, image, rest))


def reduce2_kernel(got, v2, v1, coefs, msg, rest2):
    image = reduced_halves(got)
    vec = v2[...]
    rest = image - coef(coefs, 3) * v1[...] - coef(coefs, 1) * vec
    rest2[...] = rest
    rows = [summed_tile(got, 16)[0]] + inner_rows(vec, image, rest)[1:]
    at = iota((8, W), 0)
    tile = jnp.zeros((8, W), F32)
    for k, row in enumerate(rows):
        tile = jnp.where(at == k, jnp.broadcast_to(row, (8, W)), tile)
    for n in range(CHIPS):
        msg[n] = tile


def residual_kernel(got, rest2, v2, coefs, msg, last):
    acc = got[0]
    for n in range(1, CHIPS):
        acc = acc + got[n]
    a2 = total(acc[0:1]) / COUNT
    d = a2 - coef(coefs, 1)
    put_coefs(last, (a2, d))
    rounded = (rest2[...] - d * v2[...]).astype(BF16)
    tile = split_rows([acc[k : k + 1] for k in range(1, 4)])
    half = SEC * SLAB
    for c in range(2):
        for z in range(NZ):
            msg[c * NZ + z, :half] = rounded[half * c : half * (c + 1)]
            msg[c * NZ + z, half:] = tile


def finish_kernel(got, coefs, last, vec_out, coef_out, dens_out, rest):
    vr, rr, vv, _ = half_totals(summed_tile(got, SEC * SLAB))
    a0, a1, b1, b2 = [coef(coefs, k) for k in range(4)]
    a2, d = coef(last, 0), coef(last, 1)
    norm = rr - 2.0 * d * vr + d * d * vv
    b3 = jnp.sqrt(jnp.maximum(norm, 0.0) / COUNT + EPS)
    for k, v in enumerate((a0, a1, a2, b1, b2, b3)):
        coef_out[k] = v[0, 0]
    wc = 1.0 / b3
    for s in range(GRP):
        for pair in range(SEC // 2):
            tile = got[s, 16 * pair : 16 * (pair + 1)].astype(F32)
            for k in range(2):
                rest[2 * pair + k, SLAB * s : SLAB * (s + 1), :] = tile[SLAB * k : SLAB * (k + 1)]
    for i in range(SEC):
        v = rest[i] * wc
        vec_out[i] = v
        high = v.astype(BF16)
        low = (v - high.astype(F32)).astype(BF16)
        dens_out[i] = lax.dot_general(
            jnp.concatenate([high, high, low], axis=1),
            jnp.concatenate([high, low, high], axis=1),
            (((1,), (1,)), ((), ())),
            preferred_element_type=F32,
        ) * (1.0 / W)


def over_cz(x):
    return lax.all_to_all(x, BOTH, 0, 0, axis_index_groups=CZ_GROUPS)


def over_xy(x):
    return lax.all_to_all(x, "sector", 0, 0, axis_index_groups=XY_GROUPS)


def select(got, ones):
    return call(select_kernel, [((GRP, NEAR * SLAB + 8, W), BF16)], [VMEM, VMEM])(got, ones)[0]


def per_device(theta, left, right, perm, dims):
    half = (SEC * SLAB, W)
    slab = (2 * SEC * SLAB, W)
    scatter = ((GRP, SEC * SLAB, W), BF16)
    plane = ((CHIPS, 2 * SEC * SLAB + 8, W), BF16)
    blocks = ((NBLK, W, W), F32)
    acc = [pltpu.VMEM((SEC, W, W), F32)]
    coefs = ((8, W), F32)
    flops = 2 * 2 * SEC * TERMS_DEV * W**3
    nbytes = 6 << 20

    dims = dims.T
    any_space = pl.BlockSpec(memory_space=pl.ANY)
    pieces = 2 * CHIPS
    away_type = ((2, TERMS_DEV, W, W), BF16)
    near_type = ((HELD, 2, TERMS_DEV, W, W), BF16)
    sems = pltpu.SemaphoreType.DMA((SEC + 1 + 2 * HELD,))

    msg, keep, send, limits, down, up = call(
        start_kernel,
        [((pieces, 16, W), BF16), (half, F32), (half, F32), ((8, W), jnp.int32), away_type, away_type],
        [any_space] * 4,
        [
            pltpu.VMEM((SEC, W, W), F32),
            pltpu.SMEM((2, SEC), jnp.int32),
            pltpu.VMEM(*near_type),
            sems,
            pltpu.SemaphoreType.DMA((2 * HELD,)),
        ],
        out_specs=[VMEM] * 4 + [any_space] * 2,
        limit=60,
    )(theta, dims, left, right)
    above = lax.ppermute(down, "op", DOWN)
    below = lax.ppermute(up, "op", UP)
    got = lax.all_to_all(msg, "sector", 0, 0)
    (ones,) = call(hits_kernel, [((WIDE + 2 * W // SLAB, SLAB * W), BF16)], [VMEM])(perm.reshape(1, W))
    came = lax.ppermute(send, "sector", SWAP)
    (msg,) = call(
        pick_kernel,
        [((pieces, 8 * SEC, W), BF16)],
        [VMEM, VMEM, any_space, any_space],
        [pltpu.VMEM((pieces * 16, W), F32), pltpu.VMEM((pieces * 8 * SEC, W), F32)],
    )(got, ones, came, right)
    got = lax.all_to_all(msg, "sector", 0, 0)
    msg, blk0, near = call(
        ham0_kernel,
        [scatter, blocks, near_type],
        [VMEM] * 5 + [any_space] * 2,
        acc + [pltpu.SemaphoreType.DMA((2 * HELD,))],
        flops,
        nbytes,
        limit=20,
    )(limits, theta, got, left, right, above, below)
    msg, image0, slab0 = call(reduce0_kernel, [plane, (slab, F32), (slab, F32)], [VMEM] * 3)(
        over_cz(msg), keep, came
    )

    held = ((NEAR, W, W), F32)
    acc = [pltpu.VMEM((HELD, W, W), F32)]
    got = over_cz(select(over_xy(msg), ones))
    msg, blk1, v0, v1, co = call(
        ham1_kernel,
        [((GRP, 16, W), BF16), held, (slab, F32), (slab, F32), coefs],
        [VMEM] * 8,
        acc,
        flops,
        nbytes,
        limit=20,
    )(limits, got, left, right, near, blk0, slab0, image0)
    msg, rest1 = call(reduce1_kernel, [plane, (slab, F32)], [VMEM] * 4)(over_cz(msg), v1, v0, co)

    got = over_cz(select(over_xy(msg), ones))
    msg, v2, co = call(
        ham2_kernel,
        [((GRP, 24, W), BF16), (slab, F32), coefs],
        [VMEM] * 10,
        [pltpu.VMEM((NEAR, W, W), F32)] + acc,
        flops,
        nbytes,
        limit=20,
    )(limits, got, left, right, near, blk1, blk0, v1, rest1, co)
    msg, rest2 = call(reduce2_kernel, [((CHIPS, 8, W), F32), (slab, F32)], [VMEM] * 4)(
        over_cz(msg), v2, v1, co
    )

    msg, last = call(residual_kernel, [((GRP, SEC * SLAB + 8, W), BF16), coefs], [VMEM] * 4)(
        over_xy(msg), rest2, v2, co
    )
    return call(
        finish_kernel,
        [((SEC, W, W), F32), ((6,), F32), ((SEC, W, W), F32)],
        [VMEM] * 3,
        [pltpu.VMEM((SEC, W, W), F32)],
        out_specs=[VMEM, SMEM, VMEM],
    )(over_cz(msg), co, last)


def solution(mesh):
    placed = (
        P("sector", None, None),
        P("sector", "op", None, None),
        P("sector", "op", None, None),
        P(),
        P("sector", None),
    )
    return jax.shard_map(
        per_device,
        mesh=mesh,
        in_specs=placed,
        out_specs=(P("sector", None, None), P(), P("sector", None, None)),
        check_vma=False,
    )
```

```python
import functools

import jax
import jax.numpy as jnp
from jax import lax
from jax.experimental import pallas as pl
from jax.experimental.pallas import tpu as pltpu
from jax.sharding import PartitionSpec as P

F32 = jnp.float32
BF16 = jnp.bfloat16
BOTH = ("sector", "op")
W = 128
SEC = 4
SLAB = 8
NZ = 8
CHIPS = 16
GRP = 16
NBLK = 3 * SEC
HELD = SEC // 2
NEAR = 3 * HELD
WIDE = 2 * NBLK * SLAB
TERMS_DEV = 16
COUNT = float(128 * W * W)
EPS = 1e-06
SCALE = 1.0 / (128.0**0.5)
NCOL = 4

CZ_GROUPS = [[(2 * chip + c) * NZ + z for c in range(2) for z in range(NZ)] for chip in range(CHIPS)]
XY_GROUPS = [[2 * chip + c for chip in range(CHIPS)] for c in range(2)]
SWAP = [(i, i ^ 1) for i in range(2 * CHIPS)]
DOWN = [(i, (i - 1) % NZ) for i in range(NZ)]
UP = [(i, (i + 1) % NZ) for i in range(NZ)]

VMEM = pl.BlockSpec(memory_space=pltpu.VMEM)
SMEM = pl.BlockSpec(memory_space=pltpu.SMEM)


def core_and_z():
    return lax.rem(lax.axis_index("sector"), 2), lax.axis_index("op")


def call(body, outs, specs, scratch=(), flops=0, nbytes=1 << 18, out_specs=None, limit=8):
    return pl.pallas_call(
        body,
        out_shape=[jax.ShapeDtypeStruct(s, d) for s, d in outs],
        in_specs=specs,
        out_specs=out_specs or [VMEM] * len(outs),
        scratch_shapes=list(scratch),
        compiler_params=pltpu.CompilerParams(vmem_limit_bytes=limit << 20),
        cost_estimate=pl.CostEstimate(flops=flops, bytes_accessed=nbytes, transcendentals=0),
    )


def iota(shape, dim):
    return lax.broadcasted_iota(jnp.int32, shape, dim)


def row_sum(x):
    return jnp.sum(x, axis=0, keepdims=True)


def split_rows(rows):
    left_half = iota((1, W), 1) < W // 2
    folded = [row + pltpu.roll(row, W // 2, 1) for row in rows]
    folded += [jnp.zeros((1, W), F32)] * (4 - len(rows))
    return split_again([jnp.where(left_half, folded[2 * k], folded[2 * k + 1]) for k in range(2)])


def split_again(rows):
    at = iota((8, W), 0)
    tile = jnp.zeros((8, W), F32)
    for k, row in enumerate(rows):
        hi = row.astype(BF16).astype(F32)
        mid = (row - hi).astype(BF16).astype(F32)
        low = row - hi - mid
        for n, part in enumerate((hi, mid, low)):
            tile = jnp.where(at == 3 * k + n, jnp.broadcast_to(part, (8, W)), tile)
    return tile.astype(BF16)


def join_rows(tile):
    return [row_sum(tile[3 * k : 3 * k + 3]) for k in range(2)]


def half_totals(rows):
    left_half = iota((1, W), 1) < W // 2
    out = []
    for row in rows:
        out.append(total(jnp.where(left_half, row, 0.0)))
        out.append(total(jnp.where(left_half, 0.0, row)))
    return out


def total(row):
    return jnp.sum(row, axis=1, keepdims=True)


def low_high(low, high):
    first = iota((SLAB, W), 0) < 4
    return (
        jnp.where(first, low, pltpu.roll(high, 4, 0)),
        jnp.where(first, pltpu.roll(low, 4, 0), high),
    )


def start_kernel(
    theta, dims, left, right, msg, keep, send, limits, down, up, held, sizes, stage, sems, out_sems
):
    size_copy = pltpu.make_async_copy(dims, sizes, sems.at[SEC])
    copies = [pltpu.make_async_copy(theta.at[i], held.at[i], sems.at[i]) for i in range(SEC)]
    c, z = core_and_z()
    other = HELD * (1 - lax.rem(z, 2))
    size_copy.start()
    for copy in copies:
        copy.start()
    away = (down, up)
    halves = []
    for m in range(HELD):
        for k, array in enumerate((left, right)):
            halves.append(
                (
                    pltpu.make_async_copy(array.at[other + m], stage.at[m, k], sems.at[SEC + 1 + 2 * m + k]),
                    pltpu.make_async_copy(stage.at[m, k], away[m].at[k], out_sems.at[2 * m + k]),
                )
            )
    for copy, _ in halves:
        copy.start()
    size_copy.wait()
    at = iota((8, W), 0)
    tile = jnp.zeros((8, W), jnp.int32)
    for i in range(SEC):
        for k in range(2):
            tile = jnp.where(at == 2 * i + k, sizes[k, i], tile)
    limits[...] = tile
    rows = iota((W, W), 0)
    cols = iota((W, W), 1)
    for i in range(SEC):
        copies[i].wait()
        if i == SEC - 1:
            for copy, out in halves:
                copy.wait()
                out.start()
        inside = (rows < sizes[0, i]) & (cols < sizes[1, i])
        held[i] = jnp.where(inside, held[i], 0.0)
    for t in range(GRP):
        tiles = [held[i, SLAB * t : SLAB * (t + 1), :] for i in range(SEC)]
        even0, odd0 = low_high(tiles[0], tiles[1])
        even1, odd1 = low_high(tiles[2], tiles[3])
        msg[2 * t] = jnp.concatenate([even0, even1], axis=0).astype(BF16)
        msg[2 * t + 1] = jnp.concatenate([odd0, odd1], axis=0).astype(BF16)
    for slot, out in ((c * NZ + z, keep), ((1 - c) * NZ + z, send)):
        first = pl.multiple_of(slot * SLAB, SLAB)
        for i in range(SEC):
            out[SLAB * i : SLAB * (i + 1), :] = held[i, pl.ds(first, SLAB), :]
    for _, out in halves:
        out.wait()


def wanted(perm, count, first, shift, sides):
    shape = (count, W)
    row = lax.shift_right_logical(iota(shape, 0), shift)
    if sides:
        at = lax.shift_right_logical(row, 1)
        q = 2 * lax.bitwise_and(row, 1)
    else:
        at = lax.shift_right_logical(row * 21846, 16)
        q = row - 3 * at
    held = jnp.broadcast_to(perm[...].astype(F32), shape)
    mine = jnp.sum(jnp.where(iota(shape, 1) == at + first, held, 0.0), axis=1, keepdims=True)
    want = mine + q.astype(F32) - 1.0
    want = jnp.where(want < 0.0, want + 128.0, want)
    want = jnp.where(want > 127.0, want - 128.0, want)
    return (held == want).astype(F32).astype(BF16)


def hits_kernel(perm, ones):
    hits = wanted(perm, 2 * W, 0, 0, True)
    part = 2 * W // SLAB
    for k in range(SLAB):
        ones[WIDE:, W * k : W * (k + 1)] = hits[part * k : part * (k + 1)]
    chip = lax.axis_index("sector") // 2
    near = wanted(perm, WIDE, chip * 2 * SEC, 3, False)
    cols = (W, SLAB * W)
    spread_out = (lax.shift_right_logical(iota(cols, 1), 3) == iota(cols, 0)).astype(F32).astype(BF16)
    both = jnp.dot(near, spread_out, preferred_element_type=F32)
    shape = (WIDE, SLAB * W)
    same = lax.bitwise_and(iota(shape, 0), 7) == lax.bitwise_and(iota(shape, 1), 7)
    ones[:WIDE] = jnp.where(same, both, 0.0).astype(BF16)


def pick_kernel(got, ones, came, held, msg, pieces, picked):
    for g in range(2 * CHIPS):
        pieces[16 * g : 16 * (g + 1)] = got[g].astype(F32)
    hits = jnp.concatenate([ones[WIDE:, W * k : W * (k + 1)] for k in range(SLAB)], axis=0)
    for r in range(4):
        part = pieces[pl.ds(r, W, stride=4), :].astype(BF16)
        picked[pl.ds(r, 2 * W, stride=4), :] = jnp.dot(hits, part, preferred_element_type=F32)
    for g in range(2 * CHIPS):
        msg[g] = picked[32 * g : 32 * (g + 1)].astype(BF16)


def assemble_pieces(got, theta, limits, out):
    for t in range(GRP):
        low = got[2 * t].astype(F32)
        high = got[2 * t + 1].astype(F32)
        for i in range(SEC):
            at = slice(SLAB * i, SLAB * (i + 1))
            two = low_high(low[at], high[at])
            for k in range(2):
                out[3 * i + 2 * k, SLAB * t : SLAB * (t + 1), :] = two[k]
    rows = iota((W, W), 0)
    cols = iota((W, W), 1)
    for i in range(SEC):
        inside = (rows < coef(limits, 2 * i)) & (cols < coef(limits, 2 * i + 1))
        out[3 * i + 1] = jnp.where(inside, theta[i], 0.0)


def select_kernel(shifted, got, ones, msg):
    data = 2 * SEC * SLAB
    slabs = jnp.concatenate([got[n, :data] for n in range(CHIPS)], axis=0)
    picked = jnp.dot(ones[:WIDE], slabs, preferred_element_type=F32).astype(BF16)
    acc = got[0, data:].astype(F32)
    for n in range(1, CHIPS):
        acc = acc + got[n, data:].astype(F32)
    tile = split_again(join_rows(acc))
    shifts = []
    if shifted:
        parts = []
        for n in range(CHIPS):
            row = got[n, data:].astype(F32)[6:7]
            parts += [jnp.broadcast_to(row[:, W // 2 * c : W // 2 * c + 1], (SEC * SLAB, W)) for c in range(2)]
        column = jnp.concatenate(parts, axis=0).astype(BF16)
        needed = jnp.dot(ones[:WIDE], column, preferred_element_type=F32)
        group = lax.shift_right_logical(iota((1, W), 1), 4)
        for k in range(4):
            row = jnp.zeros((1, W), F32)
            for b in range(NEAR):
                at = (NEAR * k + b) * SLAB
                row = jnp.where(group == b, needed[at : at + 1], row)
            shifts.append(jnp.where(iota((8, W), 0) == 6, row, tile.astype(F32)).astype(BF16))
    rows = NEAR * SLAB
    for c in range(2):
        for z in range(NZ):
            first = rows * (2 * c + z % 2)
            msg[c * NZ + z, :rows] = picked[first : first + rows]
            msg[c * NZ + z, rows:] = shifts[2 * c + z % 2] if shifted else tile


def summed_tile(got, first):
    acc = got[0, first:].astype(F32)
    for s in range(1, GRP):
        acc = acc + got[s, first:].astype(F32)
    return join_rows(acc)


def assemble(got, out):
    for s in range(GRP):
        for pair in range(NEAR // 2):
            tile = got[s, 16 * pair : 16 * (pair + 1)].astype(F32)
            for k in range(2):
                out[2 * pair + k, SLAB * s : SLAB * (s + 1), :] = tile[SLAB * k : SLAB * (k + 1)]


def products(limits, blocks, left, right, acc):
    _, z = core_and_z()
    rows = iota((W, W), 0)
    cols = iota((W, W), 1)
    for i in range(SEC):
        inner = []
        order = []
        for r in range(3):
            terms = list(range(r, TERMS_DEV, 3))
            vec = blocks[3 * i + lax.rem(z + r, 3)].astype(BF16)
            lhs = jnp.concatenate([left[i, w] for w in terms], axis=0)
            got = jnp.dot(lhs, vec, preferred_element_type=F32).astype(BF16)
            inner += [got[W * n : W * (n + 1)] for n in range(len(terms))]
            order += terms
        lhs = jnp.concatenate(inner, axis=1)
        rhs = jnp.concatenate([right[i, w] for w in order], axis=0)
        out = jnp.dot(lhs, rhs, preferred_element_type=F32)
        inside = (rows < coef(limits, 2 * i)) & (cols < coef(limits, 2 * i + 1))
        acc[i] = jnp.where(inside, out * SCALE, 0.0)


def pack(acc, msg):
    for s in range(GRP):
        at = slice(SLAB * s, SLAB * (s + 1))
        for pair in range(acc.shape[0] // 2):
            tile = jnp.concatenate([acc[2 * pair, at, :], acc[2 * pair + 1, at, :]], axis=0)
            msg[s, 16 * pair : 16 * (pair + 1)] = tile.astype(BF16)


def start_copies(above, below, near, sems):
    copies = []
    for m, array in enumerate((above, below)):
        for k in range(2):
            copy = pltpu.make_async_copy(array.at[k], near.at[m, k], sems.at[2 * m + k])
            copy.start()
            copies.append(copy)
    return copies


def products_held(limits, blocks, left, right, extra, acc):
    _, z = core_and_z()
    odd = lax.rem(z, 2)
    rows = iota((W, W), 0)
    cols = iota((W, W), 1)
    inner = [[], []]
    rhs = [[], []]
    for mine in (True, False):
        for m in range(HELD):
            i = HELD * odd + m
            start = z if mine else lax.rem(z + (NZ + 1 - 2 * m), NZ)
            for r in range(3):
                terms = range(r, TERMS_DEV, 3)
                vec = blocks[3 * m + lax.rem(start + r, 3)].astype(BF16)
                lhs = jnp.concatenate([left[i, w] if mine else extra[m, 0, w] for w in terms], axis=0)
                got = jnp.dot(lhs, vec, preferred_element_type=F32).astype(BF16)
                inner[m] += [got[W * n : W * (n + 1)] for n in range(len(terms))]
                rhs[m] += [right[i, w] if mine else extra[m, 1, w] for w in terms]
    for m in range(HELD):
        i = HELD * odd + m
        lhs = jnp.concatenate(inner[m], axis=1)
        out = jnp.dot(lhs, jnp.concatenate(rhs[m], axis=0), preferred_element_type=F32)
        size = limits[pl.ds(2 * i, 1), 0:1], limits[pl.ds(2 * i + 1, 1), 0:1]
        acc[m] = jnp.where((rows < size[0]) & (cols < size[1]), out * SCALE, 0.0)


def put_coefs(out, values):
    at = iota((8, W), 0)
    tile = jnp.zeros((8, W), F32)
    for k, v in enumerate(values):
        tile = jnp.where(at == k, jnp.broadcast_to(v, (8, W)), tile)
    out[...] = tile


def coef(ref, k):
    return ref[k : k + 1, 0:1]


def ham0_kernel(limits, theta, got, left, right, above, below, msg, blk, near, acc, sems):
    copies = start_copies(above, below, near, sems)
    assemble_pieces(got, theta, limits, blk)
    products(limits, blk, left, right, acc)
    uu = total(row_sum(sum(blk[3 * i + 1] * blk[3 * i + 1] for i in range(SEC))))
    up = total(row_sum(sum(blk[3 * i + 1] * acc[i] for i in range(SEC))))
    shift = jnp.where(uu > 0.0, up / jnp.where(uu > 0.0, uu, 1.0), 0.0)
    for i in range(SEC):
        acc[i] = acc[i] - shift * blk[3 * i + 1]
    pack(acc, msg)
    tile = split_again([jnp.broadcast_to(shift, (1, W))])
    for s in range(GRP):
        msg[s, SEC * SLAB :] = tile
    for copy in copies:
        copy.wait()


def ham1_kernel(
    limits, got, left, right, near, blk0, slab0, rest0, shift0, msg, blk, v0, v1, coefs, acc
):
    first = NEAR * lax.rem(core_and_z()[1], 2)
    uu, uw, ww, _ = half_totals(summed_tile(got, NEAR * SLAB))
    assemble(got, blk)
    n2 = uu / COUNT + EPS
    inv = 1.0 / jnp.sqrt(n2)
    a0 = uw / n2 / COUNT
    rr = (ww - 2.0 * a0 * uw + a0 * a0 * uu) / n2
    b1 = jnp.sqrt(jnp.maximum(rr, 0.0) / COUNT + EPS)
    wc = inv / b1
    shifts = got[0, NEAR * SLAB :].astype(F32)[6:7]
    for n in range(NEAR):
        vc = (a0 - shifts[:, 16 * n : 16 * n + 1]) * wc
        blk[n] = blk[n] * wc - blk0[first + n] * vc
    v0[...] = slab0[...] * inv
    half = SEC * SLAB
    for c in range(2):
        at = slice(half * c, half * (c + 1))
        v1[at] = rest0[at] * wc - slab0[at] * ((a0 - coef(shift0, c)) * wc)
    put_coefs(coefs, (a0, b1, inv))
    products_held(limits, blk, left, right, near, acc)
    for m in range(HELD):
        acc[m] = acc[m] - (0.25 * a0) * blk[3 * m + 1] - (0.25 * b1 * inv) * blk0[first + 3 * m + 1]
    pack(acc, msg)


def ham2_kernel(
    limits, got, left, right, near, blk1, slab1, rest1, old, msg, v2, coefs, blk, acc
):
    vw, vr, rr, vv = half_totals(summed_tile(got, NEAR * SLAB))
    assemble(got, blk)
    a0, b1 = coef(old, 0), coef(old, 1)
    a1 = vw / COUNT
    d = a1 - a0
    rest = rr - 2.0 * d * vr + d * d * vv
    b2 = jnp.sqrt(jnp.maximum(rest, 0.0) / COUNT + EPS)
    wc = 1.0 / b2
    for n in range(NEAR):
        blk[n] = blk[n] * wc - blk1[n] * (d * wc)
    v2[...] = (rest1[...] - d * slab1[...]) * wc
    put_coefs(coefs, (a0, a1, b1, b2))
    products_held(limits, blk, left, right, near, acc)
    dots = row_sum(sum(blk[3 * m + 1] * acc[m] for m in range(HELD)))
    for m in range(HELD):
        acc[m] = acc[m] - (0.25 * a1) * blk[3 * m + 1] - (0.25 * b2) * blk1[3 * m + 1]
    pack(acc, msg)
    tile = split_rows([dots])
    for s in range(GRP):
        msg[s, 16:] = tile


def reduced(got):
    data = SEC * SLAB
    out = []
    for c in range(2):
        acc = got[c * NZ].astype(F32)
        for z in range(1, NZ):
            acc = acc + got[c * NZ + z].astype(F32)
        out.append((acc[:data], row_sum(acc[data : data + 3])))
    return out


def reduced_halves(got):
    parts = []
    for c in range(2):
        for odd in range(2):
            acc = got[c * NZ + odd, :16].astype(F32)
            for z in range(odd + 2, NZ, 2):
                acc = acc + got[c * NZ + z, :16].astype(F32)
            parts.append(acc)
    return jnp.concatenate(parts, axis=0)


def spread(msg, image, rows, extra=None):
    data = 2 * SEC * SLAB
    rounded = image.astype(BF16)
    tile = split_rows(rows)
    if extra is not None:
        tile = jnp.where(iota((8, W), 0) == 6, extra, tile.astype(F32)).astype(BF16)
    for n in range(CHIPS):
        msg[n, :data] = rounded
        msg[n, data:] = tile


def reduce0_kernel(got, keep, came, msg, rest0, slab0, shift0):
    c, _ = core_and_z()
    half = SEC * SLAB
    slab0[:half] = jnp.where(c == 0, keep[...], came[...])
    slab0[half:] = jnp.where(c == 0, came[...], keep[...])
    image = []
    shifts = []
    for k, (acc, shift) in enumerate(reduced(got)):
        at = slice(half * k, half * (k + 1))
        sent = shift.astype(BF16).astype(F32)
        rest0[at] = acc + (shift - sent) * slab0[at]
        image.append(acc + shift * slab0[at])
        shifts.append(sent)
    put_coefs(shift0, [row[:, 0:1] for row in shifts])
    vec = slab0[...]
    image = jnp.concatenate(image, axis=0)
    rows = [row_sum(vec * vec), row_sum(vec * image), row_sum(image * image)]
    spread(msg, rest0[...], rows, jnp.where(iota((1, W), 1) < W // 2, shifts[0], shifts[1]))


def inner_rows(vec, image, rest):
    return [row_sum(vec * image), row_sum(vec * rest), row_sum(rest * rest), row_sum(vec * vec)]


def reduce1_kernel(got, v1, v0, coefs, msg, rest1):
    rest = reduced_halves(got)
    vec = v1[...]
    image = rest + coef(coefs, 1) * v0[...] + coef(coefs, 0) * vec
    rest1[...] = rest
    spread(msg, rest, inner_rows(vec, image, rest))


def reduce2_kernel(got, v2, msg, rest2):
    rest = reduced_halves(got)
    vec = v2[...]
    rest2[...] = rest
    rows = [summed_tile(got, 16)[0], row_sum(vec * rest), row_sum(rest * rest), row_sum(vec * vec)]
    at = iota((8, W), 0)
    tile = jnp.zeros((8, W), F32)
    for k, row in enumerate(rows):
        tile = jnp.where(at == k, jnp.broadcast_to(row, (8, W)), tile)
    for n in range(CHIPS):
        msg[n] = tile


def residual_kernel(got, rest2, v2, coefs, msg, last):
    acc = got[0]
    for n in range(1, CHIPS):
        acc = acc + got[n]
    a2 = total(acc[0:1]) / COUNT
    d = a2 - coef(coefs, 1)
    put_coefs(last, (a2, d))
    rounded = (rest2[...] - d * v2[...]).astype(BF16)
    tile = split_rows([acc[k : k + 1] for k in range(1, 4)])
    half = SEC * SLAB
    for c in range(2):
        for z in range(NZ):
            msg[c * NZ + z, :half] = rounded[half * c : half * (c + 1)]
            msg[c * NZ + z, half:] = tile


def finish_kernel(got, coefs, last, vec_out, coef_out, dens_out, rest):
    vr, rr, vv, _ = half_totals(summed_tile(got, SEC * SLAB))
    a0, a1, b1, b2 = [coef(coefs, k) for k in range(4)]
    a2, d = coef(last, 0), coef(last, 1)
    norm = rr - 2.0 * d * vr + d * d * vv
    b3 = jnp.sqrt(jnp.maximum(norm, 0.0) / COUNT + EPS)
    for k, v in enumerate((a0, a1, a2, b1, b2, b3)):
        coef_out[k] = v[0, 0]
    wc = 1.0 / b3
    for s in range(GRP):
        for pair in range(SEC // 2):
            tile = got[s, 16 * pair : 16 * (pair + 1)].astype(F32)
            for k in range(2):
                rest[2 * pair + k, SLAB * s : SLAB * (s + 1), :] = tile[SLAB * k : SLAB * (k + 1)]
    for i in range(SEC):
        v = rest[i] * wc
        vec_out[i] = v
        high = v.astype(BF16)
        low = (v - high.astype(F32)).astype(BF16)
        dens_out[i] = lax.dot_general(
            jnp.concatenate([high, high, low], axis=1),
            jnp.concatenate([high, low, high], axis=1),
            (((1,), (1,)), ((), ())),
            preferred_element_type=F32,
        ) * (1.0 / W)


def over_cz(x):
    return lax.all_to_all(x, BOTH, 0, 0, axis_index_groups=CZ_GROUPS)


def over_xy(x):
    return lax.all_to_all(x, "sector", 0, 0, axis_index_groups=XY_GROUPS)


def select(shifted, got, ones):
    return call(
        functools.partial(select_kernel, shifted), [((GRP, NEAR * SLAB + 8, W), BF16)], [VMEM, VMEM])(got, ones)[0]


def per_device(theta, left, right, perm, dims):
    half = (SEC * SLAB, W)
    slab = (2 * SEC * SLAB, W)
    scatter = ((GRP, SEC * SLAB + 8, W), BF16)
    plane = ((CHIPS, 2 * SEC * SLAB + 8, W), BF16)
    blocks = ((NBLK, W, W), F32)
    acc = [pltpu.VMEM((SEC, W, W), F32)]
    coefs = ((8, W), F32)
    flops = 2 * 2 * SEC * TERMS_DEV * W**3
    nbytes = 6 << 20

    dims = dims.T
    any_space = pl.BlockSpec(memory_space=pl.ANY)
    pieces = 2 * CHIPS
    away_type = ((2, TERMS_DEV, W, W), BF16)
    near_type = ((HELD, 2, TERMS_DEV, W, W), BF16)
    sems = pltpu.SemaphoreType.DMA((SEC + 1 + 2 * HELD,))

    msg, keep, send, limits, down, up = call(
        start_kernel,
        [((pieces, 16, W), BF16), (half, F32), (half, F32), ((8, W), jnp.int32), away_type, away_type],
        [any_space] * 4,
        [
            pltpu.VMEM((SEC, W, W), F32),
            pltpu.SMEM((2, SEC), jnp.int32),
            pltpu.VMEM(*near_type),
            sems,
            pltpu.SemaphoreType.DMA((2 * HELD,)),
        ],
        out_specs=[VMEM] * 4 + [any_space] * 2,
        limit=60,
    )(theta, dims, left, right)
    above = lax.ppermute(down, "op", DOWN)
    below = lax.ppermute(up, "op", UP)
    got = lax.all_to_all(msg, "sector", 0, 0)
    (ones,) = call(hits_kernel, [((WIDE + 2 * W // SLAB, SLAB * W), BF16)], [VMEM])(perm.reshape(1, W))
    came = lax.ppermute(send, "sector", SWAP)
    (msg,) = call(
        pick_kernel,
        [((pieces, 8 * SEC, W), BF16)],
        [VMEM, VMEM, any_space, any_space],
        [pltpu.VMEM((pieces * 16, W), F32), pltpu.VMEM((pieces * 8 * SEC, W), F32)],
    )(got, ones, came, right)
    got = lax.all_to_all(msg, "sector", 0, 0)
    msg, blk0, near = call(
        ham0_kernel,
        [scatter, blocks, near_type],
        [VMEM] * 5 + [any_space] * 2,
        acc + [pltpu.SemaphoreType.DMA((2 * HELD,))],
        flops,
        nbytes,
        limit=20,
    )(limits, theta, got, left, right, above, below)
    msg, rest0, slab0, shift0 = call(
        reduce0_kernel, [plane, (slab, F32), (slab, F32), coefs], [VMEM] * 3
    )(
        over_cz(msg), keep, came
    )

    held = ((NEAR, W, W), F32)
    acc = [pltpu.VMEM((HELD, W, W), F32)]
    got = over_cz(select(True, over_xy(msg), ones))
    msg, blk1, v0, v1, co = call(
        ham1_kernel,
        [((GRP, 16, W), BF16), held, (slab, F32), (slab, F32), coefs],
        [VMEM] * 9,
        acc,
        flops,
        nbytes,
        limit=20,
    )(limits, got, left, right, near, blk0, slab0, rest0, shift0)
    msg, rest1 = call(reduce1_kernel, [plane, (slab, F32)], [VMEM] * 4)(over_cz(msg), v1, v0, co)

    got = over_cz(select(False, over_xy(msg), ones))
    msg, v2, co = call(
        ham2_kernel,
        [((GRP, 24, W), BF16), (slab, F32), coefs],
        [VMEM] * 9,
        [pltpu.VMEM((NEAR, W, W), F32)] + acc,
        flops,
        nbytes,
        limit=20,
    )(limits, got, left, right, near, blk1, v1, rest1, co)
    msg, rest2 = call(reduce2_kernel, [((CHIPS, 8, W), F32), (slab, F32)], [VMEM] * 2)(
        over_cz(msg), v2
    )

    msg, last = call(residual_kernel, [((GRP, SEC * SLAB + 8, W), BF16), coefs], [VMEM] * 4)(
        over_xy(msg), rest2, v2, co
    )
    return call(
        finish_kernel,
        [((SEC, W, W), F32), ((6,), F32), ((SEC, W, W), F32)],
        [VMEM] * 3,
        [pltpu.VMEM((SEC, W, W), F32)],
        out_specs=[VMEM, SMEM, VMEM],
    )(over_cz(msg), co, last)


def solution(mesh):
    placed = (
        P("sector", None, None),
        P("sector", "op", None, None),
        P("sector", "op", None, None),
        P(),
        P("sector", None),
    )
    return jax.shard_map(
        per_device,
        mesh=mesh,
        in_specs=placed,
        out_specs=(P("sector", None, None), P(), P("sector", None, None)),
        check_vma=False,
    )
```

```python
import functools

import jax
import jax.numpy as jnp
from jax import lax
from jax.experimental import pallas as pl
from jax.experimental.pallas import tpu as pltpu
from jax.sharding import PartitionSpec as P

F32 = jnp.float32
BF16 = jnp.bfloat16
BOTH = ("sector", "op")
W = 128
SEC = 4
SLAB = 8
NZ = 8
CHIPS = 16
GRP = 16
NBLK = 3 * SEC
HELD = SEC // 2
NEAR = 3 * HELD
WIDE = 2 * NBLK * SLAB
TERMS_DEV = 16
COUNT = float(128 * W * W)
EPS = 1e-06
SCALE = 1.0 / (128.0**0.5)
NCOL = 4

CZ_GROUPS = [[(2 * chip + c) * NZ + z for c in range(2) for z in range(NZ)] for chip in range(CHIPS)]
XY_GROUPS = [[2 * chip + c for chip in range(CHIPS)] for c in range(2)]
SWAP = [(i, i ^ 1) for i in range(2 * CHIPS)]
DOWN = [(i, (i - 1) % NZ) for i in range(NZ)]
UP = [(i, (i + 1) % NZ) for i in range(NZ)]

VMEM = pl.BlockSpec(memory_space=pltpu.VMEM)
SMEM = pl.BlockSpec(memory_space=pltpu.SMEM)


def core_and_z():
    return lax.rem(lax.axis_index("sector"), 2), lax.axis_index("op")


def call(body, outs, specs, scratch=(), flops=0, nbytes=1 << 18, out_specs=None, limit=8):
    return pl.pallas_call(
        body,
        out_shape=[jax.ShapeDtypeStruct(s, d) for s, d in outs],
        in_specs=specs,
        out_specs=out_specs or [VMEM] * len(outs),
        scratch_shapes=list(scratch),
        compiler_params=pltpu.CompilerParams(vmem_limit_bytes=limit << 20),
        cost_estimate=pl.CostEstimate(flops=flops, bytes_accessed=nbytes, transcendentals=0),
    )


def iota(shape, dim):
    return lax.broadcasted_iota(jnp.int32, shape, dim)


def row_sum(x):
    return jnp.sum(x, axis=0, keepdims=True)


def split_rows(rows):
    left_half = iota((1, W), 1) < W // 2
    folded = [row + pltpu.roll(row, W // 2, 1) for row in rows]
    folded += [jnp.zeros((1, W), F32)] * (4 - len(rows))
    return split_again([jnp.where(left_half, folded[2 * k], folded[2 * k + 1]) for k in range(2)])


def split_again(rows):
    at = iota((8, W), 0)
    tile = jnp.zeros((8, W), F32)
    for k, row in enumerate(rows):
        hi = row.astype(BF16).astype(F32)
        mid = (row - hi).astype(BF16).astype(F32)
        low = row - hi - mid
        for n, part in enumerate((hi, mid, low)):
            tile = jnp.where(at == 3 * k + n, jnp.broadcast_to(part, (8, W)), tile)
    return tile.astype(BF16)


def join_rows(tile):
    return [row_sum(tile[3 * k : 3 * k + 3]) for k in range(2)]


def half_totals(rows):
    left_half = iota((1, W), 1) < W // 2
    out = []
    for row in rows:
        out.append(total(jnp.where(left_half, row, 0.0)))
        out.append(total(jnp.where(left_half, 0.0, row)))
    return out


def total(row):
    return jnp.sum(row, axis=1, keepdims=True)


def low_high(low, high):
    first = iota((SLAB, W), 0) < 4
    return (
        jnp.where(first, low, pltpu.roll(high, 4, 0)),
        jnp.where(first, pltpu.roll(low, 4, 0), high),
    )


def start_kernel(
    theta, dims, left, right, msg, keep, send, limits, down, up, held, sizes, stage, sems, out_sems
):
    size_copy = pltpu.make_async_copy(dims, sizes, sems.at[SEC])
    copies = [pltpu.make_async_copy(theta.at[i], held.at[i], sems.at[i]) for i in range(SEC)]
    c, z = core_and_z()
    other = HELD * (1 - lax.rem(z, 2))
    size_copy.start()
    for copy in copies:
        copy.start()
    away = (down, up)
    halves = []
    for m in range(HELD):
        for k, array in enumerate((left, right)):
            halves.append(
                (
                    pltpu.make_async_copy(array.at[other + m], stage.at[m, k], sems.at[SEC + 1 + 2 * m + k]),
                    pltpu.make_async_copy(stage.at[m, k], away[m].at[k], out_sems.at[2 * m + k]),
                )
            )
    for copy, _ in halves:
        copy.start()
    size_copy.wait()
    at = iota((8, W), 0)
    tile = jnp.zeros((8, W), jnp.int32)
    for i in range(SEC):
        for k in range(2):
            tile = jnp.where(at == 2 * i + k, sizes[k, i], tile)
    limits[...] = tile
    rows = iota((W, W), 0)
    cols = iota((W, W), 1)
    for i in range(SEC):
        copies[i].wait()
        if i == SEC - 1:
            for copy, out in halves:
                copy.wait()
                out.start()
        inside = (rows < sizes[0, i]) & (cols < sizes[1, i])
        held[i] = jnp.where(inside, held[i], 0.0)
    for t in range(GRP):
        tiles = [held[i, SLAB * t : SLAB * (t + 1), :] for i in range(SEC)]
        even0, odd0 = low_high(tiles[0], tiles[1])
        even1, odd1 = low_high(tiles[2], tiles[3])
        msg[2 * t] = jnp.concatenate([even0, even1], axis=0).astype(BF16)
        msg[2 * t + 1] = jnp.concatenate([odd0, odd1], axis=0).astype(BF16)
    for slot, out in ((c * NZ + z, keep), ((1 - c) * NZ + z, send)):
        first = pl.multiple_of(slot * SLAB, SLAB)
        for i in range(SEC):
            out[SLAB * i : SLAB * (i + 1), :] = held[i, pl.ds(first, SLAB), :]
    for _, out in halves:
        out.wait()


def wanted(perm, count, first, shift, sides):
    shape = (count, W)
    row = lax.shift_right_logical(iota(shape, 0), shift)
    if sides:
        at = lax.shift_right_logical(row, 1)
        q = 2 * lax.bitwise_and(row, 1)
    else:
        at = lax.shift_right_logical(row * 21846, 16)
        q = row - 3 * at
    held = jnp.broadcast_to(perm[...].astype(F32), shape)
    mine = jnp.sum(jnp.where(iota(shape, 1) == at + first, held, 0.0), axis=1, keepdims=True)
    want = mine + q.astype(F32) - 1.0
    want = jnp.where(want < 0.0, want + 128.0, want)
    want = jnp.where(want > 127.0, want - 128.0, want)
    return (held == want).astype(F32).astype(BF16)


def hits_kernel(perm, ones):
    hits = wanted(perm, 2 * W, 0, 0, True)
    part = 2 * W // SLAB
    for k in range(SLAB):
        ones[WIDE:, W * k : W * (k + 1)] = hits[part * k : part * (k + 1)]
    chip = lax.axis_index("sector") // 2
    near = wanted(perm, WIDE, chip * 2 * SEC, 3, False)
    cols = (W, SLAB * W)
    spread_out = (lax.shift_right_logical(iota(cols, 1), 3) == iota(cols, 0)).astype(F32).astype(BF16)
    both = jnp.dot(near, spread_out, preferred_element_type=F32)
    shape = (WIDE, SLAB * W)
    same = lax.bitwise_and(iota(shape, 0), 7) == lax.bitwise_and(iota(shape, 1), 7)
    ones[:WIDE] = jnp.where(same, both, 0.0).astype(BF16)


def pick_kernel(got, ones, came, held, msg, pieces, picked):
    for g in range(2 * CHIPS):
        pieces[16 * g : 16 * (g + 1)] = got[g].astype(F32)
    hits = jnp.concatenate([ones[WIDE:, W * k : W * (k + 1)] for k in range(SLAB)], axis=0)
    for r in range(4):
        part = pieces[pl.ds(r, W, stride=4), :].astype(BF16)
        picked[pl.ds(r, 2 * W, stride=4), :] = jnp.dot(hits, part, preferred_element_type=F32)
    for g in range(2 * CHIPS):
        msg[g] = picked[32 * g : 32 * (g + 1)].astype(BF16)


def assemble_pieces(got, theta, limits, out):
    for t in range(GRP):
        low = got[2 * t].astype(F32)
        high = got[2 * t + 1].astype(F32)
        for i in range(SEC):
            at = slice(SLAB * i, SLAB * (i + 1))
            two = low_high(low[at], high[at])
            for k in range(2):
                out[3 * i + 2 * k, SLAB * t : SLAB * (t + 1), :] = two[k]
    rows = iota((W, W), 0)
    cols = iota((W, W), 1)
    for i in range(SEC):
        inside = (rows < coef(limits, 2 * i)) & (cols < coef(limits, 2 * i + 1))
        out[3 * i + 1] = jnp.where(inside, theta[i], 0.0)


def select_kernel(shifted, got, ones, msg):
    data = 2 * SEC * SLAB
    slabs = jnp.concatenate([got[n, :data] for n in range(CHIPS)], axis=0)
    picked = jnp.dot(ones[:WIDE], slabs, preferred_element_type=F32).astype(BF16)
    acc = got[0, data:].astype(F32)
    for n in range(1, CHIPS):
        acc = acc + got[n, data:].astype(F32)
    tile = split_again(join_rows(acc))
    shifts = []
    if shifted:
        parts = []
        for n in range(CHIPS):
            row = got[n, data:].astype(F32)[6:7]
            parts += [jnp.broadcast_to(row[:, W // 2 * c : W // 2 * c + 1], (SEC * SLAB, W)) for c in range(2)]
        column = jnp.concatenate(parts, axis=0).astype(BF16)
        needed = jnp.dot(ones[:WIDE], column, preferred_element_type=F32)
        group = lax.shift_right_logical(iota((1, W), 1), 4)
        for k in range(4):
            row = jnp.zeros((1, W), F32)
            for b in range(NEAR):
                at = (NEAR * k + b) * SLAB
                row = jnp.where(group == b, needed[at : at + 1], row)
            shifts.append(jnp.where(iota((8, W), 0) == 6, row, tile.astype(F32)).astype(BF16))
    rows = NEAR * SLAB
    for c in range(2):
        for z in range(NZ):
            first = rows * (2 * c + z % 2)
            msg[c * NZ + z, :rows] = picked[first : first + rows]
            msg[c * NZ + z, rows:] = shifts[2 * c + z % 2] if shifted else tile


def summed_tile(got, first):
    acc = got[0, first:].astype(F32)
    for s in range(1, GRP):
        acc = acc + got[s, first:].astype(F32)
    return join_rows(acc)


def assemble(got, out):
    for s in range(GRP):
        for pair in range(NEAR // 2):
            tile = got[s, 16 * pair : 16 * (pair + 1)].astype(F32)
            for k in range(2):
                out[2 * pair + k, SLAB * s : SLAB * (s + 1), :] = tile[SLAB * k : SLAB * (k + 1)]


def products(limits, blocks, left, right, acc):
    _, z = core_and_z()
    rows = iota((W, W), 0)
    cols = iota((W, W), 1)
    for i in range(SEC):
        inner = []
        order = []
        for r in range(3):
            terms = list(range(r, TERMS_DEV, 3))
            vec = blocks[3 * i + lax.rem(z + r, 3)].astype(BF16)
            lhs = jnp.concatenate([left[i, w] for w in terms], axis=0)
            got = jnp.dot(lhs, vec, preferred_element_type=F32).astype(BF16)
            inner += [got[W * n : W * (n + 1)] for n in range(len(terms))]
            order += terms
        lhs = jnp.concatenate(inner, axis=1)
        rhs = jnp.concatenate([right[i, w] for w in order], axis=0)
        out = jnp.dot(lhs, rhs, preferred_element_type=F32)
        inside = (rows < coef(limits, 2 * i)) & (cols < coef(limits, 2 * i + 1))
        acc[i] = jnp.where(inside, out * SCALE, 0.0)


def pack(count, rows, msg):
    for s in range(GRP):
        at = slice(SLAB * s, SLAB * (s + 1))
        for pair in range(count // 2):
            tile = jnp.concatenate([rows(2 * pair, at), rows(2 * pair + 1, at)], axis=0)
            msg[s, 16 * pair : 16 * (pair + 1)] = tile.astype(BF16)


def start_copies(above, below, near, sems):
    copies = []
    for m, array in enumerate((above, below)):
        for k in range(2):
            copy = pltpu.make_async_copy(array.at[k], near.at[m, k], sems.at[2 * m + k])
            copy.start()
            copies.append(copy)
    return copies


def products_held(limits, blocks, left, right, extra, acc):
    _, z = core_and_z()
    odd = lax.rem(z, 2)
    rows = iota((W, W), 0)
    cols = iota((W, W), 1)
    inner = [[], []]
    rhs = [[], []]
    for mine in (True, False):
        for m in range(HELD):
            i = HELD * odd + m
            start = z if mine else lax.rem(z + (NZ + 1 - 2 * m), NZ)
            for r in range(3):
                terms = range(r, TERMS_DEV, 3)
                vec = blocks[3 * m + lax.rem(start + r, 3)].astype(BF16)
                lhs = jnp.concatenate([left[i, w] if mine else extra[m, 0, w] for w in terms], axis=0)
                got = jnp.dot(lhs, vec, preferred_element_type=F32).astype(BF16)
                inner[m] += [got[W * n : W * (n + 1)] for n in range(len(terms))]
                rhs[m] += [right[i, w] if mine else extra[m, 1, w] for w in terms]
    for m in range(HELD):
        i = HELD * odd + m
        lhs = jnp.concatenate(inner[m], axis=1)
        out = jnp.dot(lhs, jnp.concatenate(rhs[m], axis=0), preferred_element_type=F32)
        size = limits[pl.ds(2 * i, 1), 0:1], limits[pl.ds(2 * i + 1, 1), 0:1]
        acc[m] = jnp.where((rows < size[0]) & (cols < size[1]), out * SCALE, 0.0)


def put_coefs(out, values):
    at = iota((8, W), 0)
    tile = jnp.zeros((8, W), F32)
    for k, v in enumerate(values):
        tile = jnp.where(at == k, jnp.broadcast_to(v, (8, W)), tile)
    out[...] = tile


def coef(ref, k):
    return ref[k : k + 1, 0:1]


def ham0_kernel(limits, theta, got, left, right, above, below, msg, blk, near, acc, sems):
    copies = start_copies(above, below, near, sems)
    assemble_pieces(got, theta, limits, blk)
    products(limits, blk, left, right, acc)
    uu = total(row_sum(sum(blk[3 * i + 1] * blk[3 * i + 1] for i in range(SEC))))
    up = total(row_sum(sum(blk[3 * i + 1] * acc[i] for i in range(SEC))))
    shift = jnp.where(uu > 0.0, up / jnp.where(uu > 0.0, uu, 1.0), 0.0)
    pack(SEC, lambda i, at: acc[i, at, :] - shift * blk[3 * i + 1, at, :], msg)
    tile = split_again([jnp.broadcast_to(shift, (1, W))])
    for s in range(GRP):
        msg[s, SEC * SLAB :] = tile
    for copy in copies:
        copy.wait()


def ham1_kernel(
    limits, got, left, right, near, blk0, slab0, rest0, shift0, msg, blk, v0, v1, coefs, acc
):
    first = NEAR * lax.rem(core_and_z()[1], 2)
    uu, uw, ww, _ = half_totals(summed_tile(got, NEAR * SLAB))
    assemble(got, blk)
    n2 = uu / COUNT + EPS
    inv = 1.0 / jnp.sqrt(n2)
    a0 = uw / n2 / COUNT
    rr = (ww - 2.0 * a0 * uw + a0 * a0 * uu) / n2
    b1 = jnp.sqrt(jnp.maximum(rr, 0.0) / COUNT + EPS)
    wc = inv / b1
    shifts = got[0, NEAR * SLAB :].astype(F32)[6:7]
    for n in range(NEAR):
        vc = (a0 - shifts[:, 16 * n : 16 * n + 1]) * wc
        blk[n] = blk[n] * wc - blk0[first + n] * vc
    v0[...] = slab0[...] * inv
    half = SEC * SLAB
    for c in range(2):
        at = slice(half * c, half * (c + 1))
        v1[at] = rest0[at] * wc - slab0[at] * ((a0 - coef(shift0, c)) * wc)
    put_coefs(coefs, (a0, b1, inv))
    products_held(limits, blk, left, right, near, acc)
    share, before = 0.25 * a0, 0.25 * b1 * inv
    pack(
        HELD,
        lambda m, at: acc[m, at, :]
        - share * blk[3 * m + 1, at, :]
        - before * blk0[first + 3 * m + 1, at, :],
        msg,
    )


def ham2_kernel(
    limits, got, left, right, near, blk1, slab1, rest1, old, msg, v2, coefs, blk, acc
):
    vw, vr, rr, vv = half_totals(summed_tile(got, NEAR * SLAB))
    assemble(got, blk)
    a0, b1 = coef(old, 0), coef(old, 1)
    a1 = vw / COUNT
    d = a1 - a0
    rest = rr - 2.0 * d * vr + d * d * vv
    b2 = jnp.sqrt(jnp.maximum(rest, 0.0) / COUNT + EPS)
    wc = 1.0 / b2
    for n in range(NEAR):
        blk[n] = blk[n] * wc - blk1[n] * (d * wc)
    v2[...] = (rest1[...] - d * slab1[...]) * wc
    put_coefs(coefs, (a0, a1, b1, b2))
    products_held(limits, blk, left, right, near, acc)
    dots = row_sum(sum(blk[3 * m + 1] * acc[m] for m in range(HELD)))
    share, before = 0.25 * a1, 0.25 * b2
    pack(
        HELD,
        lambda m, at: acc[m, at, :] - share * blk[3 * m + 1, at, :] - before * blk1[3 * m + 1, at, :],
        msg,
    )
    tile = split_rows([dots])
    for s in range(GRP):
        msg[s, 16:] = tile


def reduced(got):
    data = SEC * SLAB
    out = []
    for c in range(2):
        acc = got[c * NZ].astype(F32)
        for z in range(1, NZ):
            acc = acc + got[c * NZ + z].astype(F32)
        out.append((acc[:data], row_sum(acc[data : data + 3])))
    return out


def reduced_halves(got):
    parts = []
    for c in range(2):
        for odd in range(2):
            acc = got[c * NZ + odd, :16].astype(F32)
            for z in range(odd + 2, NZ, 2):
                acc = acc + got[c * NZ + z, :16].astype(F32)
            parts.append(acc)
    return jnp.concatenate(parts, axis=0)


def spread(msg, image, rows, extra=None):
    data = 2 * SEC * SLAB
    rounded = image.astype(BF16)
    tile = split_rows(rows)
    if extra is not None:
        tile = jnp.where(iota((8, W), 0) == 6, extra, tile.astype(F32)).astype(BF16)
    for n in range(CHIPS):
        msg[n, :data] = rounded
        msg[n, data:] = tile


def reduce0_kernel(got, keep, came, msg, rest0, slab0, shift0):
    c, _ = core_and_z()
    half = SEC * SLAB
    slab0[:half] = jnp.where(c == 0, keep[...], came[...])
    slab0[half:] = jnp.where(c == 0, came[...], keep[...])
    image = []
    shifts = []
    for k, (acc, shift) in enumerate(reduced(got)):
        at = slice(half * k, half * (k + 1))
        sent = shift.astype(BF16).astype(F32)
        rest0[at] = acc + (shift - sent) * slab0[at]
        image.append(acc + shift * slab0[at])
        shifts.append(sent)
    put_coefs(shift0, [row[:, 0:1] for row in shifts])
    vec = slab0[...]
    image = jnp.concatenate(image, axis=0)
    rows = [row_sum(vec * vec), row_sum(vec * image), row_sum(image * image)]
    spread(msg, rest0[...], rows, jnp.where(iota((1, W), 1) < W // 2, shifts[0], shifts[1]))


def inner_rows(vec, image, rest):
    return [row_sum(vec * image), row_sum(vec * rest), row_sum(rest * rest), row_sum(vec * vec)]


def reduce1_kernel(got, v1, v0, coefs, msg, rest1):
    rest = reduced_halves(got)
    vec = v1[...]
    image = rest + coef(coefs, 1) * v0[...] + coef(coefs, 0) * vec
    rest1[...] = rest
    spread(msg, rest, inner_rows(vec, image, rest))


def reduce2_kernel(got, v2, msg, rest2):
    rest = reduced_halves(got)
    vec = v2[...]
    rest2[...] = rest
    rows = [summed_tile(got, 16)[0], row_sum(vec * rest), row_sum(rest * rest), row_sum(vec * vec)]
    at = iota((8, W), 0)
    tile = jnp.zeros((8, W), F32)
    for k, row in enumerate(rows):
        tile = jnp.where(at == k, jnp.broadcast_to(row, (8, W)), tile)
    for n in range(CHIPS):
        msg[n] = tile


def residual_kernel(got, rest2, v2, coefs, msg, last):
    acc = got[0]
    for n in range(1, CHIPS):
        acc = acc + got[n]
    a2 = total(acc[0:1]) / COUNT
    d = a2 - coef(coefs, 1)
    put_coefs(last, (a2, d))
    rounded = (rest2[...] - d * v2[...]).astype(BF16)
    tile = split_rows([acc[k : k + 1] for k in range(1, 4)])
    half = SEC * SLAB
    for c in range(2):
        for z in range(NZ):
            msg[c * NZ + z, :half] = rounded[half * c : half * (c + 1)]
            msg[c * NZ + z, half:] = tile


def finish_kernel(got, coefs, last, vec_out, coef_out, dens_out, rest, dens, sems):
    copies = []
    vr, rr, vv, _ = half_totals(summed_tile(got, SEC * SLAB))
    a0, a1, b1, b2 = [coef(coefs, k) for k in range(4)]
    a2, d = coef(last, 0), coef(last, 1)
    norm = rr - 2.0 * d * vr + d * d * vv
    b3 = jnp.sqrt(jnp.maximum(norm, 0.0) / COUNT + EPS)
    for k, v in enumerate((a0, a1, a2, b1, b2, b3)):
        coef_out[k] = v[0, 0]
    wc = 1.0 / b3
    for s in range(GRP):
        for pair in range(SEC // 2):
            tile = got[s, 16 * pair : 16 * (pair + 1)].astype(F32)
            for k in range(2):
                rest[2 * pair + k, SLAB * s : SLAB * (s + 1), :] = tile[SLAB * k : SLAB * (k + 1)]
    for i in range(SEC):
        v = rest[i] * wc
        rest[i] = v
        copies.append(pltpu.make_async_copy(rest.at[i], vec_out.at[i], sems.at[i]))
        copies[-1].start()
        high = v.astype(BF16)
        low = (v - high.astype(F32)).astype(BF16)
        dens[i] = lax.dot_general(
            jnp.concatenate([high, high, low], axis=1),
            jnp.concatenate([high, low, high], axis=1),
            (((1,), (1,)), ((), ())),
            preferred_element_type=F32,
        ) * (1.0 / W)
        copies.append(pltpu.make_async_copy(dens.at[i], dens_out.at[i], sems.at[SEC + i]))
        copies[-1].start()
    for copy in copies:
        copy.wait()


def over_cz(x):
    return lax.all_to_all(x, BOTH, 0, 0, axis_index_groups=CZ_GROUPS)


def over_xy(x):
    return lax.all_to_all(x, "sector", 0, 0, axis_index_groups=XY_GROUPS)


def select(shifted, got, ones):
    return call(
        functools.partial(select_kernel, shifted), [((GRP, NEAR * SLAB + 8, W), BF16)], [VMEM, VMEM])(got, ones)[0]


def per_device(theta, left, right, perm, dims):
    half = (SEC * SLAB, W)
    slab = (2 * SEC * SLAB, W)
    scatter = ((GRP, SEC * SLAB + 8, W), BF16)
    plane = ((CHIPS, 2 * SEC * SLAB + 8, W), BF16)
    blocks = ((NBLK, W, W), F32)
    acc = [pltpu.VMEM((SEC, W, W), F32)]
    coefs = ((8, W), F32)
    flops = 2 * 2 * SEC * TERMS_DEV * W**3
    nbytes = 6 << 20

    dims = dims.T
    any_space = pl.BlockSpec(memory_space=pl.ANY)
    pieces = 2 * CHIPS
    away_type = ((2, TERMS_DEV, W, W), BF16)
    near_type = ((HELD, 2, TERMS_DEV, W, W), BF16)
    sems = pltpu.SemaphoreType.DMA((SEC + 1 + 2 * HELD,))

    msg, keep, send, limits, down, up = call(
        start_kernel,
        [((pieces, 16, W), BF16), (half, F32), (half, F32), ((8, W), jnp.int32), away_type, away_type],
        [any_space] * 4,
        [
            pltpu.VMEM((SEC, W, W), F32),
            pltpu.SMEM((2, SEC), jnp.int32),
            pltpu.VMEM(*near_type),
            sems,
            pltpu.SemaphoreType.DMA((2 * HELD,)),
        ],
        out_specs=[VMEM] * 4 + [any_space] * 2,
        limit=60,
    )(theta, dims, left, right)
    above = lax.ppermute(down, "op", DOWN)
    below = lax.ppermute(up, "op", UP)
    got = lax.all_to_all(msg, "sector", 0, 0)
    (ones,) = call(hits_kernel, [((WIDE + 2 * W // SLAB, SLAB * W), BF16)], [VMEM])(perm.reshape(1, W))
    came = lax.ppermute(send, "sector", SWAP)
    (msg,) = call(
        pick_kernel,
        [((pieces, 8 * SEC, W), BF16)],
        [VMEM, VMEM, any_space, any_space],
        [pltpu.VMEM((pieces * 16, W), F32), pltpu.VMEM((pieces * 8 * SEC, W), F32)],
    )(got, ones, came, right)
    got = lax.all_to_all(msg, "sector", 0, 0)
    msg, blk0, near = call(
        ham0_kernel,
        [scatter, blocks, near_type],
        [VMEM] * 5 + [any_space] * 2,
        acc + [pltpu.SemaphoreType.DMA((2 * HELD,))],
        flops,
        nbytes,
        limit=20,
    )(limits, theta, got, left, right, above, below)
    msg, rest0, slab0, shift0 = call(
        reduce0_kernel, [plane, (slab, F32), (slab, F32), coefs], [VMEM] * 3
    )(
        over_cz(msg), keep, came
    )

    held = ((NEAR, W, W), F32)
    acc = [pltpu.VMEM((HELD, W, W), F32)]
    got = over_cz(select(True, over_xy(msg), ones))
    msg, blk1, v0, v1, co = call(
        ham1_kernel,
        [((GRP, 16, W), BF16), held, (slab, F32), (slab, F32), coefs],
        [VMEM] * 9,
        acc,
        flops,
        nbytes,
        limit=20,
    )(limits, got, left, right, near, blk0, slab0, rest0, shift0)
    msg, rest1 = call(reduce1_kernel, [plane, (slab, F32)], [VMEM] * 4)(over_cz(msg), v1, v0, co)

    got = over_cz(select(False, over_xy(msg), ones))
    msg, v2, co = call(
        ham2_kernel,
        [((GRP, 24, W), BF16), (slab, F32), coefs],
        [VMEM] * 9,
        [pltpu.VMEM((NEAR, W, W), F32)] + acc,
        flops,
        nbytes,
        limit=20,
    )(limits, got, left, right, near, blk1, v1, rest1, co)
    msg, rest2 = call(reduce2_kernel, [((CHIPS, 8, W), F32), (slab, F32)], [VMEM] * 2)(
        over_cz(msg), v2
    )

    msg, last = call(residual_kernel, [((GRP, SEC * SLAB + 8, W), BF16), coefs], [VMEM] * 4)(
        over_xy(msg), rest2, v2, co
    )
    return call(
        finish_kernel,
        [((SEC, W, W), F32), ((6,), F32), ((SEC, W, W), F32)],
        [VMEM] * 3,
        [pltpu.VMEM((SEC, W, W), F32)] * 2 + [pltpu.SemaphoreType.DMA((2 * SEC,))],
        out_specs=[any_space, SMEM, any_space],
    )(over_cz(msg), co, last)


def solution(mesh):
    placed = (
        P("sector", None, None),
        P("sector", "op", None, None),
        P("sector", "op", None, None),
        P(),
        P("sector", None),
    )
    return jax.shard_map(
        per_device,
        mesh=mesh,
        in_specs=placed,
        out_specs=(P("sector", None, None), P(), P("sector", None, None)),
        check_vma=False,
    )
```

```python
import functools

import jax
import jax.numpy as jnp
from jax import lax
from jax.experimental import pallas as pl
from jax.experimental.pallas import tpu as pltpu
from jax.sharding import PartitionSpec as P

F32 = jnp.float32
BF16 = jnp.bfloat16
BOTH = ("sector", "op")
W = 128
SEC = 4
SLAB = 8
NZ = 8
CHIPS = 16
GRP = 16
NBLK = 3 * SEC
HELD = SEC // 2
NEAR = 3 * HELD
WIDE = 2 * NBLK * SLAB
TERMS_DEV = 16
COUNT = float(128 * W * W)
EPS = 1e-06
SCALE = 1.0 / (128.0**0.5)
NCOL = 4

CZ_GROUPS = [[(2 * chip + c) * NZ + z for c in range(2) for z in range(NZ)] for chip in range(CHIPS)]
XY_GROUPS = [[2 * chip + c for chip in range(CHIPS)] for c in range(2)]
SWAP = [(i, i ^ 1) for i in range(2 * CHIPS)]
DOWN = [(i, (i - 1) % NZ) for i in range(NZ)]
UP = [(i, (i + 1) % NZ) for i in range(NZ)]

VMEM = pl.BlockSpec(memory_space=pltpu.VMEM)
SMEM = pl.BlockSpec(memory_space=pltpu.SMEM)


def core_and_z():
    return lax.rem(lax.axis_index("sector"), 2), lax.axis_index("op")


def call(body, outs, specs, scratch=(), flops=0, nbytes=1 << 18, out_specs=None, limit=8):
    return pl.pallas_call(
        body,
        out_shape=[jax.ShapeDtypeStruct(s, d) for s, d in outs],
        in_specs=specs,
        out_specs=out_specs or [VMEM] * len(outs),
        scratch_shapes=list(scratch),
        compiler_params=pltpu.CompilerParams(vmem_limit_bytes=limit << 20),
        cost_estimate=pl.CostEstimate(flops=flops, bytes_accessed=nbytes, transcendentals=0),
    )


def iota(shape, dim):
    return lax.broadcasted_iota(jnp.int32, shape, dim)


def row_sum(x):
    return jnp.sum(x, axis=0, keepdims=True)


def split_rows(rows):
    left_half = iota((1, W), 1) < W // 2
    folded = [row + pltpu.roll(row, W // 2, 1) for row in rows]
    folded += [jnp.zeros((1, W), F32)] * (4 - len(rows))
    return split_again([jnp.where(left_half, folded[2 * k], folded[2 * k + 1]) for k in range(2)])


def split_again(rows):
    at = iota((8, W), 0)
    tile = jnp.zeros((8, W), F32)
    for k, row in enumerate(rows):
        hi = row.astype(BF16).astype(F32)
        mid = (row - hi).astype(BF16).astype(F32)
        low = row - hi - mid
        for n, part in enumerate((hi, mid, low)):
            tile = jnp.where(at == 3 * k + n, jnp.broadcast_to(part, (8, W)), tile)
    return tile.astype(BF16)


def join_rows(tile):
    return [row_sum(tile[3 * k : 3 * k + 3]) for k in range(2)]


def half_totals(rows):
    left_half = iota((1, W), 1) < W // 2
    out = []
    for row in rows:
        out.append(total(jnp.where(left_half, row, 0.0)))
        out.append(total(jnp.where(left_half, 0.0, row)))
    return out


def total(row):
    return jnp.sum(row, axis=1, keepdims=True)


def low_high(low, high):
    first = iota((SLAB, W), 0) < 4
    return (
        jnp.where(first, low, pltpu.roll(high, 4, 0)),
        jnp.where(first, pltpu.roll(low, 4, 0), high),
    )


def start_kernel(
    theta, dims, left, right, msg, keep, send, limits, down, up, held, sizes, stage, sems, out_sems
):
    size_copy = pltpu.make_async_copy(dims, sizes, sems.at[SEC])
    copies = [pltpu.make_async_copy(theta.at[i], held.at[i], sems.at[i]) for i in range(SEC)]
    c, z = core_and_z()
    other = HELD * (1 - lax.rem(z, 2))
    size_copy.start()
    for copy in copies:
        copy.start()
    away = (down, up)
    halves = []
    for m in range(HELD):
        for k, array in enumerate((left, right)):
            halves.append(
                (
                    pltpu.make_async_copy(array.at[other + m], stage.at[m, k], sems.at[SEC + 1 + 2 * m + k]),
                    pltpu.make_async_copy(stage.at[m, k], away[m].at[k], out_sems.at[2 * m + k]),
                )
            )
    for copy, _ in halves:
        copy.start()
    size_copy.wait()
    at = iota((8, W), 0)
    tile = jnp.zeros((8, W), jnp.int32)
    for i in range(SEC):
        for k in range(2):
            tile = jnp.where(at == 2 * i + k, sizes[k, i], tile)
    limits[...] = tile
    rows = iota((W, W), 0)
    cols = iota((W, W), 1)
    for i in range(SEC):
        copies[i].wait()
        if i == SEC - 1:
            for copy, out in halves:
                copy.wait()
                out.start()
        inside = (rows < sizes[0, i]) & (cols < sizes[1, i])
        held[i] = jnp.where(inside, held[i], 0.0)
    for t in range(GRP):
        tiles = [held[i, SLAB * t : SLAB * (t + 1), :] for i in range(SEC)]
        even0, odd0 = low_high(tiles[0], tiles[1])
        even1, odd1 = low_high(tiles[2], tiles[3])
        msg[2 * t] = jnp.concatenate([even0, even1], axis=0).astype(BF16)
        msg[2 * t + 1] = jnp.concatenate([odd0, odd1], axis=0).astype(BF16)
    for slot, out in ((c * NZ + z, keep), ((1 - c) * NZ + z, send)):
        first = pl.multiple_of(slot * SLAB, SLAB)
        for i in range(SEC):
            out[SLAB * i : SLAB * (i + 1), :] = held[i, pl.ds(first, SLAB), :]
    for _, out in halves:
        out.wait()


def wanted(perm, count, first, shift, sides):
    shape = (count, W)
    row = lax.shift_right_logical(iota(shape, 0), shift)
    if sides:
        at = lax.shift_right_logical(row, 1)
        q = 2 * lax.bitwise_and(row, 1)
    else:
        at = lax.shift_right_logical(row * 21846, 16)
        q = row - 3 * at
    held = jnp.broadcast_to(perm[...].astype(F32), shape)
    mine = jnp.sum(jnp.where(iota(shape, 1) == at + first, held, 0.0), axis=1, keepdims=True)
    want = mine + q.astype(F32) - 1.0
    want = jnp.where(want < 0.0, want + 128.0, want)
    want = jnp.where(want > 127.0, want - 128.0, want)
    return (held == want).astype(F32).astype(BF16)


def hits_kernel(perm, ones):
    hits = wanted(perm, 2 * W, 0, 0, True)
    part = 2 * W // SLAB
    for k in range(SLAB):
        ones[WIDE:, W * k : W * (k + 1)] = hits[part * k : part * (k + 1)]
    chip = lax.axis_index("sector") // 2
    near = wanted(perm, WIDE, chip * 2 * SEC, 3, False)
    cols = (W, SLAB * W)
    spread_out = (lax.shift_right_logical(iota(cols, 1), 3) == iota(cols, 0)).astype(F32).astype(BF16)
    both = jnp.dot(near, spread_out, preferred_element_type=F32)
    shape = (WIDE, SLAB * W)
    same = lax.bitwise_and(iota(shape, 0), 7) == lax.bitwise_and(iota(shape, 1), 7)
    ones[:WIDE] = jnp.where(same, both, 0.0).astype(BF16)


def pick_kernel(got, ones, came, held, msg, pieces, picked):
    for g in range(2 * CHIPS):
        pieces[16 * g : 16 * (g + 1)] = got[g].astype(F32)
    hits = jnp.concatenate([ones[WIDE:, W * k : W * (k + 1)] for k in range(SLAB)], axis=0)
    for r in range(4):
        part = pieces[pl.ds(r, W, stride=4), :].astype(BF16)
        picked[pl.ds(r, 2 * W, stride=4), :] = jnp.dot(hits, part, preferred_element_type=F32)
    for g in range(2 * CHIPS):
        msg[g] = picked[32 * g : 32 * (g + 1)].astype(BF16)


def assemble_pieces(got, theta, limits, out):
    for t in range(GRP):
        low = got[2 * t].astype(F32)
        high = got[2 * t + 1].astype(F32)
        for i in range(SEC):
            at = slice(SLAB * i, SLAB * (i + 1))
            two = low_high(low[at], high[at])
            for k in range(2):
                out[3 * i + 2 * k, SLAB * t : SLAB * (t + 1), :] = two[k]
    rows = iota((W, W), 0)
    cols = iota((W, W), 1)
    for i in range(SEC):
        inside = (rows < coef(limits, 2 * i)) & (cols < coef(limits, 2 * i + 1))
        out[3 * i + 1] = jnp.where(inside, theta[i], 0.0)


def select_kernel(shifted, got, ones, msg):
    data = 2 * SEC * SLAB
    slabs = jnp.concatenate([got[n, :data] for n in range(CHIPS)], axis=0)
    picked = jnp.dot(ones[:WIDE], slabs, preferred_element_type=F32).astype(BF16)
    acc = got[0, data:].astype(F32)
    for n in range(1, CHIPS):
        acc = acc + got[n, data:].astype(F32)
    tile = split_again(join_rows(acc))
    shifts = []
    if shifted:
        parts = []
        for n in range(CHIPS):
            row = got[n, data:].astype(F32)[6:7]
            parts += [jnp.broadcast_to(row[:, W // 2 * c : W // 2 * c + 1], (SEC * SLAB, W)) for c in range(2)]
        column = jnp.concatenate(parts, axis=0).astype(BF16)
        needed = jnp.dot(ones[:WIDE], column, preferred_element_type=F32)
        group = lax.shift_right_logical(iota((1, W), 1), 4)
        for k in range(4):
            row = jnp.zeros((1, W), F32)
            for b in range(NEAR):
                at = (NEAR * k + b) * SLAB
                row = jnp.where(group == b, needed[at : at + 1], row)
            shifts.append(jnp.where(iota((8, W), 0) == 6, row, tile.astype(F32)).astype(BF16))
    rows = NEAR * SLAB
    for c in range(2):
        for z in range(NZ):
            first = rows * (2 * c + z % 2)
            msg[c * NZ + z, :rows] = picked[first : first + rows]
            msg[c * NZ + z, rows:] = shifts[2 * c + z % 2] if shifted else tile


def summed_tile(got, first):
    acc = got[0, first:].astype(F32)
    for s in range(1, GRP):
        acc = acc + got[s, first:].astype(F32)
    return join_rows(acc)


def assemble(got, out):
    for s in range(GRP):
        for pair in range(NEAR // 2):
            tile = got[s, 16 * pair : 16 * (pair + 1)].astype(F32)
            for k in range(2):
                out[2 * pair + k, SLAB * s : SLAB * (s + 1), :] = tile[SLAB * k : SLAB * (k + 1)]


def products(limits, blocks, left, right, acc):
    own = along = jnp.zeros((1, W), F32)
    _, z = core_and_z()
    rows = iota((W, W), 0)
    cols = iota((W, W), 1)
    for i in range(SEC):
        inner = []
        order = []
        for r in range(3):
            terms = list(range(r, TERMS_DEV, 3))
            vec = blocks[3 * i + lax.rem(z + r, 3)].astype(BF16)
            lhs = jnp.concatenate([left[i, w] for w in terms], axis=0)
            got = jnp.dot(lhs, vec, preferred_element_type=F32).astype(BF16)
            inner += [got[W * n : W * (n + 1)] for n in range(len(terms))]
            order += terms
        lhs = jnp.concatenate(inner, axis=1)
        rhs = jnp.concatenate([right[i, w] for w in order], axis=0)
        out = jnp.dot(lhs, rhs, preferred_element_type=F32)
        inside = (rows < coef(limits, 2 * i)) & (cols < coef(limits, 2 * i + 1))
        out = jnp.where(inside, out * SCALE, 0.0)
        acc[i] = out
        vec = blocks[3 * i + 1]
        own = own + row_sum(vec * vec)
        along = along + row_sum(vec * out)
    return total(own), total(along)


def pack(count, rows, msg):
    for s in range(GRP):
        at = slice(SLAB * s, SLAB * (s + 1))
        for pair in range(count // 2):
            tile = jnp.concatenate([rows(2 * pair, at), rows(2 * pair + 1, at)], axis=0)
            msg[s, 16 * pair : 16 * (pair + 1)] = tile.astype(BF16)


def start_copies(above, below, near, sems):
    copies = []
    for m, array in enumerate((above, below)):
        for k in range(2):
            copy = pltpu.make_async_copy(array.at[k], near.at[m, k], sems.at[2 * m + k])
            copy.start()
            copies.append(copy)
    return copies


def products_held(limits, blocks, left, right, extra, acc):
    _, z = core_and_z()
    odd = lax.rem(z, 2)
    rows = iota((W, W), 0)
    cols = iota((W, W), 1)
    inner = [[], []]
    rhs = [[], []]
    for mine in (True, False):
        for m in range(HELD):
            i = HELD * odd + m
            start = z if mine else lax.rem(z + (NZ + 1 - 2 * m), NZ)
            for r in range(3):
                terms = range(r, TERMS_DEV, 3)
                vec = blocks[3 * m + lax.rem(start + r, 3)].astype(BF16)
                lhs = jnp.concatenate([left[i, w] if mine else extra[m, 0, w] for w in terms], axis=0)
                got = jnp.dot(lhs, vec, preferred_element_type=F32).astype(BF16)
                inner[m] += [got[W * n : W * (n + 1)] for n in range(len(terms))]
                rhs[m] += [right[i, w] if mine else extra[m, 1, w] for w in terms]
    for m in range(HELD):
        i = HELD * odd + m
        lhs = jnp.concatenate(inner[m], axis=1)
        out = jnp.dot(lhs, jnp.concatenate(rhs[m], axis=0), preferred_element_type=F32)
        size = limits[pl.ds(2 * i, 1), 0:1], limits[pl.ds(2 * i + 1, 1), 0:1]
        acc[m] = jnp.where((rows < size[0]) & (cols < size[1]), out * SCALE, 0.0)


def put_coefs(out, values):
    at = iota((8, W), 0)
    tile = jnp.zeros((8, W), F32)
    for k, v in enumerate(values):
        tile = jnp.where(at == k, jnp.broadcast_to(v, (8, W)), tile)
    out[...] = tile


def coef(ref, k):
    return ref[k : k + 1, 0:1]


def ham0_kernel(limits, theta, got, left, right, above, below, msg, blk, near, acc, sems):
    copies = start_copies(above, below, near, sems)
    assemble_pieces(got, theta, limits, blk)
    uu, up = products(limits, blk, left, right, acc)
    shift = jnp.where(uu > 0.0, up / jnp.where(uu > 0.0, uu, 1.0), 0.0)
    pack(SEC, lambda i, at: acc[i, at, :] - shift * blk[3 * i + 1, at, :], msg)
    tile = split_again([jnp.broadcast_to(shift, (1, W))])
    for s in range(GRP):
        msg[s, SEC * SLAB :] = tile
    for copy in copies:
        copy.wait()


def ham1_kernel(
    limits, got, left, right, near, blk0, slab0, rest0, shift0, msg, blk, v0, v1, coefs, acc
):
    first = NEAR * lax.rem(core_and_z()[1], 2)
    uu, uw, ww, _ = half_totals(summed_tile(got, NEAR * SLAB))
    assemble(got, blk)
    n2 = uu / COUNT + EPS
    inv = 1.0 / jnp.sqrt(n2)
    a0 = uw / n2 / COUNT
    rr = (ww - 2.0 * a0 * uw + a0 * a0 * uu) / n2
    b1 = jnp.sqrt(jnp.maximum(rr, 0.0) / COUNT + EPS)
    wc = inv / b1
    shifts = got[0, NEAR * SLAB :].astype(F32)[6:7]
    for n in range(NEAR):
        vc = (a0 - shifts[:, 16 * n : 16 * n + 1]) * wc
        blk[n] = blk[n] * wc - blk0[first + n] * vc
    v0[...] = slab0[...] * inv
    half = SEC * SLAB
    for c in range(2):
        at = slice(half * c, half * (c + 1))
        v1[at] = rest0[at] * wc - slab0[at] * ((a0 - coef(shift0, c)) * wc)
    put_coefs(coefs, (a0, b1, inv))
    products_held(limits, blk, left, right, near, acc)
    share, before = 0.25 * a0, 0.25 * b1 * inv
    pack(
        HELD,
        lambda m, at: acc[m, at, :]
        - share * blk[3 * m + 1, at, :]
        - before * blk0[first + 3 * m + 1, at, :],
        msg,
    )


def ham2_kernel(
    limits, got, left, right, near, blk1, slab1, rest1, old, msg, v2, coefs, blk, acc
):
    vw, vr, rr, vv = half_totals(summed_tile(got, NEAR * SLAB))
    assemble(got, blk)
    a0, b1 = coef(old, 0), coef(old, 1)
    a1 = vw / COUNT
    d = a1 - a0
    rest = rr - 2.0 * d * vr + d * d * vv
    b2 = jnp.sqrt(jnp.maximum(rest, 0.0) / COUNT + EPS)
    wc = 1.0 / b2
    for n in range(NEAR):
        blk[n] = blk[n] * wc - blk1[n] * (d * wc)
    v2[...] = (rest1[...] - d * slab1[...]) * wc
    put_coefs(coefs, (a0, a1, b1, b2))
    products_held(limits, blk, left, right, near, acc)
    dots = row_sum(sum(blk[3 * m + 1] * acc[m] for m in range(HELD)))
    share, before = 0.25 * a1, 0.25 * b2
    pack(
        HELD,
        lambda m, at: acc[m, at, :] - share * blk[3 * m + 1, at, :] - before * blk1[3 * m + 1, at, :],
        msg,
    )
    tile = split_rows([dots])
    for s in range(GRP):
        msg[s, 16:] = tile


def reduced(got):
    data = SEC * SLAB
    out = []
    for c in range(2):
        acc = got[c * NZ].astype(F32)
        for z in range(1, NZ):
            acc = acc + got[c * NZ + z].astype(F32)
        out.append((acc[:data], row_sum(acc[data : data + 3])))
    return out


def reduced_halves(got):
    parts = []
    for c in range(2):
        for odd in range(2):
            acc = got[c * NZ + odd, :16].astype(F32)
            for z in range(odd + 2, NZ, 2):
                acc = acc + got[c * NZ + z, :16].astype(F32)
            parts.append(acc)
    return jnp.concatenate(parts, axis=0)


def spread(msg, image, rows, extra=None):
    data = 2 * SEC * SLAB
    rounded = image.astype(BF16)
    tile = split_rows(rows)
    if extra is not None:
        tile = jnp.where(iota((8, W), 0) == 6, extra, tile.astype(F32)).astype(BF16)
    for n in range(CHIPS):
        msg[n, :data] = rounded
        msg[n, data:] = tile


def reduce0_kernel(got, keep, came, msg, rest0, slab0, shift0):
    c, _ = core_and_z()
    half = SEC * SLAB
    slab0[:half] = jnp.where(c == 0, keep[...], came[...])
    slab0[half:] = jnp.where(c == 0, came[...], keep[...])
    image = []
    shifts = []
    for k, (acc, shift) in enumerate(reduced(got)):
        at = slice(half * k, half * (k + 1))
        sent = shift.astype(BF16).astype(F32)
        rest0[at] = acc + (shift - sent) * slab0[at]
        image.append(acc + shift * slab0[at])
        shifts.append(sent)
    put_coefs(shift0, [row[:, 0:1] for row in shifts])
    vec = slab0[...]
    image = jnp.concatenate(image, axis=0)
    rows = [row_sum(vec * vec), row_sum(vec * image), row_sum(image * image)]
    spread(msg, rest0[...], rows, jnp.where(iota((1, W), 1) < W // 2, shifts[0], shifts[1]))


def inner_rows(vec, image, rest):
    return [row_sum(vec * image), row_sum(vec * rest), row_sum(rest * rest), row_sum(vec * vec)]


def reduce1_kernel(got, v1, v0, coefs, msg, rest1):
    rest = reduced_halves(got)
    vec = v1[...]
    image = rest + coef(coefs, 1) * v0[...] + coef(coefs, 0) * vec
    rest1[...] = rest
    spread(msg, rest, inner_rows(vec, image, rest))


def reduce2_kernel(got, v2, msg, rest2):
    rest = reduced_halves(got)
    vec = v2[...]
    rest2[...] = rest
    rows = [summed_tile(got, 16)[0], row_sum(vec * rest), row_sum(rest * rest), row_sum(vec * vec)]
    at = iota((8, W), 0)
    tile = jnp.zeros((8, W), F32)
    for k, row in enumerate(rows):
        tile = jnp.where(at == k, jnp.broadcast_to(row, (8, W)), tile)
    for n in range(CHIPS):
        msg[n] = tile


def residual_kernel(got, rest2, v2, coefs, msg, last):
    acc = got[0]
    for n in range(1, CHIPS):
        acc = acc + got[n]
    a2 = total(acc[0:1]) / COUNT
    d = a2 - coef(coefs, 1)
    put_coefs(last, (a2, d))
    rounded = (rest2[...] - d * v2[...]).astype(BF16)
    tile = split_rows([acc[k : k + 1] for k in range(1, 4)])
    half = SEC * SLAB
    for c in range(2):
        for z in range(NZ):
            msg[c * NZ + z, :half] = rounded[half * c : half * (c + 1)]
            msg[c * NZ + z, half:] = tile


def finish_kernel(got, coefs, last, vec_out, coef_out, dens_out, rest):
    vr, rr, vv, _ = half_totals(summed_tile(got, SEC * SLAB))
    a0, a1, b1, b2 = [coef(coefs, k) for k in range(4)]
    a2, d = coef(last, 0), coef(last, 1)
    norm = rr - 2.0 * d * vr + d * d * vv
    b3 = jnp.sqrt(jnp.maximum(norm, 0.0) / COUNT + EPS)
    for k, v in enumerate((a0, a1, a2, b1, b2, b3)):
        coef_out[k] = v[0, 0]
    wc = 1.0 / b3
    for s in range(GRP):
        for pair in range(SEC // 2):
            tile = got[s, 16 * pair : 16 * (pair + 1)].astype(F32)
            for k in range(2):
                rest[2 * pair + k, SLAB * s : SLAB * (s + 1), :] = tile[SLAB * k : SLAB * (k + 1)]
    for i in range(SEC):
        v = rest[i] * wc
        vec_out[i] = v
        high = v.astype(BF16)
        low = (v - high.astype(F32)).astype(BF16)
        dens_out[i] = lax.dot_general(
            jnp.concatenate([high, high, low], axis=1),
            jnp.concatenate([high, low, high], axis=1),
            (((1,), (1,)), ((), ())),
            preferred_element_type=F32,
        ) * (1.0 / W)


def over_cz(x):
    return lax.all_to_all(x, BOTH, 0, 0, axis_index_groups=CZ_GROUPS)


def over_xy(x):
    return lax.all_to_all(x, "sector", 0, 0, axis_index_groups=XY_GROUPS)


def select(shifted, got, ones):
    return call(
        functools.partial(select_kernel, shifted), [((GRP, NEAR * SLAB + 8, W), BF16)], [VMEM, VMEM])(got, ones)[0]


def per_device(theta, left, right, perm, dims):
    half = (SEC * SLAB, W)
    slab = (2 * SEC * SLAB, W)
    scatter = ((GRP, SEC * SLAB + 8, W), BF16)
    plane = ((CHIPS, 2 * SEC * SLAB + 8, W), BF16)
    blocks = ((NBLK, W, W), F32)
    acc = [pltpu.VMEM((SEC, W, W), F32)]
    coefs = ((8, W), F32)
    flops = 2 * 2 * SEC * TERMS_DEV * W**3
    nbytes = 6 << 20

    dims = dims.T
    any_space = pl.BlockSpec(memory_space=pl.ANY)
    pieces = 2 * CHIPS
    away_type = ((2, TERMS_DEV, W, W), BF16)
    near_type = ((HELD, 2, TERMS_DEV, W, W), BF16)
    sems = pltpu.SemaphoreType.DMA((SEC + 1 + 2 * HELD,))

    msg, keep, send, limits, down, up = call(
        start_kernel,
        [((pieces, 16, W), BF16), (half, F32), (half, F32), ((8, W), jnp.int32), away_type, away_type],
        [any_space] * 4,
        [
            pltpu.VMEM((SEC, W, W), F32),
            pltpu.SMEM((2, SEC), jnp.int32),
            pltpu.VMEM(*near_type),
            sems,
            pltpu.SemaphoreType.DMA((2 * HELD,)),
        ],
        out_specs=[VMEM] * 4 + [any_space] * 2,
        limit=60,
    )(theta, dims, left, right)
    above = lax.ppermute(down, "op", DOWN)
    below = lax.ppermute(up, "op", UP)
    got = lax.all_to_all(msg, "sector", 0, 0)
    (ones,) = call(hits_kernel, [((WIDE + 2 * W // SLAB, SLAB * W), BF16)], [VMEM])(perm.reshape(1, W))
    came = lax.ppermute(send, "sector", SWAP)
    (msg,) = call(
        pick_kernel,
        [((pieces, 8 * SEC, W), BF16)],
        [VMEM, VMEM, any_space, any_space],
        [pltpu.VMEM((pieces * 16, W), F32), pltpu.VMEM((pieces * 8 * SEC, W), F32)],
    )(got, ones, came, right)
    got = lax.all_to_all(msg, "sector", 0, 0)
    msg, blk0, near = call(
        ham0_kernel,
        [scatter, blocks, near_type],
        [VMEM] * 5 + [any_space] * 2,
        acc + [pltpu.SemaphoreType.DMA((2 * HELD,))],
        flops,
        nbytes,
        limit=20,
    )(limits, theta, got, left, right, above, below)
    msg, rest0, slab0, shift0 = call(
        reduce0_kernel, [plane, (slab, F32), (slab, F32), coefs], [VMEM] * 3
    )(
        over_cz(msg), keep, came
    )

    held = ((NEAR, W, W), F32)
    acc = [pltpu.VMEM((HELD, W, W), F32)]
    got = over_cz(select(True, over_xy(msg), ones))
    msg, blk1, v0, v1, co = call(
        ham1_kernel,
        [((GRP, 16, W), BF16), held, (slab, F32), (slab, F32), coefs],
        [VMEM] * 9,
        acc,
        flops,
        nbytes,
        limit=20,
    )(limits, got, left, right, near, blk0, slab0, rest0, shift0)
    msg, rest1 = call(reduce1_kernel, [plane, (slab, F32)], [VMEM] * 4)(over_cz(msg), v1, v0, co)

    got = over_cz(select(False, over_xy(msg), ones))
    msg, v2, co = call(
        ham2_kernel,
        [((GRP, 24, W), BF16), (slab, F32), coefs],
        [VMEM] * 9,
        [pltpu.VMEM((NEAR, W, W), F32)] + acc,
        flops,
        nbytes,
        limit=20,
    )(limits, got, left, right, near, blk1, v1, rest1, co)
    msg, rest2 = call(reduce2_kernel, [((CHIPS, 8, W), F32), (slab, F32)], [VMEM] * 2)(
        over_cz(msg), v2
    )

    msg, last = call(residual_kernel, [((GRP, SEC * SLAB + 8, W), BF16), coefs], [VMEM] * 4)(
        over_xy(msg), rest2, v2, co
    )
    return call(
        finish_kernel,
        [((SEC, W, W), F32), ((6,), F32), ((SEC, W, W), F32)],
        [VMEM] * 3,
        [pltpu.VMEM((SEC, W, W), F32)],
        out_specs=[VMEM, SMEM, VMEM],
    )(over_cz(msg), co, last)


def solution(mesh):
    placed = (
        P("sector", None, None),
        P("sector", "op", None, None),
        P("sector", "op", None, None),
        P(),
        P("sector", None),
    )
    return jax.shard_map(
        per_device,
        mesh=mesh,
        in_specs=placed,
        out_specs=(P("sector", None, None), P(), P("sector", None, None)),
        check_vma=False,
    )
```
